32 devices in a mesh: seq: 8 (over y, x, core), tp: 4 (over z).
Axes of the slice: x: 2, y: 2, z: 4, core: 2. Of those that a mesh axis runs over, the one named last changes fastest.
Arguments:
- hidden: bfloat16 [2048, 1024], P('seq'), may hold values from -6 to 6
- segment_ids: int32 [2048], replicated, may hold values from 0 to 3, never falling along the last dimension, each value on 1 to 1536 neighbouring positions
- routes: int32 [2048, 8], P('seq'), may hold values from 0 to 31, all different within a row; in each aligned block of 256 rows (0 to 255, 256 to 511, ...) at most 128 rows name the same one
- gates: float32 [2048, 8], P('seq'), may hold values from 0.02 to 0.25
- norm_attn: bfloat16 [1024], replicated, may hold values from 0.5 to 1.5
- norm_moe: bfloat16 [1024], replicated, may hold values from 0.5 to 1.5
- w_query: bfloat16 [1024, 1024], P(None, 'tp')
- w_key: bfloat16 [1024, 512], P(None, 'tp')
- w_value: bfloat16 [1024, 512], P(None, 'tp'), may hold values from -0.1875 to 0.1875
- w_out: bfloat16 [1024, 1024], P('tp'), may hold values from -1 to 1
- w_gate: bfloat16 [32, 1024, 512], P('seq', None, 'tp'), as said below
- w_up: bfloat16 [32, 1024, 512], P('seq', None, 'tp'), as said below
- w_down: bfloat16 [32, 512, 1024], P('seq', 'tp'), as said below
Outputs:
- hidden_out: bfloat16 [2048, 1024], P('seq')
- kv_cache: bfloat16 [2048, 2, 512], P('seq', None, 'tp')
The draws below stay inside these ranges and needn't reach their ends.
Inputs may be any that keep to these rules, and one draw needn't show every extreme that they name: `segment_ids`: segment numbers start at 0, never fall and rise by one at each new segment; no segment is longer than 1536 tokens and one has exactly 1536. `routes`: each row names 8 different experts. In each aligned block of 256 rows no expert is named by more than 128 rows, a bound that some block reaches. Slot s holds the weights of expert s mod 32: w_gate[s] equals w_gate[s mod 32]. w_up[s] equals w_up[s mod 32]. w_down[s] equals w_down[s mod 32].
All inputs are finite; a program needn't handle non-finite values.
Results may differ from the reference program's by a relative error of at most 0.018.
Values may be sent and summed in bfloat16 or wider, within the bound.
A program may use at most 64 MiB of HBM per device.

```python
import math
import jax
import jax.numpy as jnp
import numpy as np
from jax import lax

D = 1024
HEADS = 16
KV_HEADS = 8
HEAD_DIM = 64
EXPERTS = 32
FF = 512
TOPK = 8
TOK_DEV = 256
TOKENS = 2048
SLOTS = 32
COPIES = 1
CAP = 128
SEG_MAX = 1536
SEGS = 4
N_TP = 4


def expert_table(key, rows, cols, fan):
    base = jax.random.normal(key, (EXPERTS, rows, cols), jnp.float32) * fan ** (-0.5)
    return jnp.tile(base, (SLOTS // EXPERTS, 1, 1)).astype(jnp.bfloat16)


def draw_w_gate(key, part):
    return expert_table(jax.random.fold_in(key, 11), D, FF, D)


def draw_w_up(key, part):
    return expert_table(jax.random.fold_in(key, 23), D, FF, D)


def draw_w_down(key, part):
    return expert_table(jax.random.fold_in(key, 37), FF, D, FF)


def draw_hidden(key, part):
    values = jnp.clip(jax.random.normal(jax.random.fold_in(key, 1), (TOKENS, D), jnp.float32), -6.0, 6.0)
    return values.astype(jnp.bfloat16)


def drawn_projection(key, salt, columns):
    values = jax.random.normal(jax.random.fold_in(key, salt), (D, columns), jnp.float32) * D ** (-0.5) * 2.0
    return values.astype(jnp.bfloat16)


def draw_w_query(key, part):
    return drawn_projection(key, 41, HEADS * HEAD_DIM)


def draw_w_key(key, part):
    return drawn_projection(key, 53, KV_HEADS * HEAD_DIM)


def shard_levels(rng, dims, cuts, smallest, high):
    def one(dim, parts):
        heights = jax.random.uniform(jax.random.fold_in(jax.random.fold_in(rng, 6), dim), (parts,), jnp.float32, smallest / len(cuts), high / len(cuts))
        return jnp.repeat(jnp.exp(heights), dims[dim] // parts).reshape((-1,) + (1,) * (len(dims) - dim - 1))

    factor_of = one(*cuts[0])
    for cut in cuts[1:]:
        factor_of = factor_of * one(*cut)
    return factor_of


def length_profile(number_of, total, limit, lean):
    loads = [(1 << 20) // math.isqrt(rank ** lean) + 1 for rank in range(2, number_of + 1)]
    spare, holding = total - limit - (number_of - 1), [1] * (number_of - 1)
    while spare > 0:
        candidates = [i for i in range(number_of - 1) if holding[i] < limit]
        pool, left = sum([loads[i] for i in candidates]), spare
        for i in candidates:
            extra = min(limit - holding[i], max(1, left * loads[i] // pool), spare)
            holding[i] = holding[i] + extra
            spare = spare - extra
    return np.array([limit] + holding)


def uneven_parts(stream_key, amount, total, most, slope):
    if amount == 2:
        one = jax.random.randint(stream_key, (), max(1, total - most), min(most, total - 1) + 1)
        return jnp.stack([one, total - one])
    sizes = jnp.asarray(length_profile(amount, total, most, slope), jnp.int32)
    twos = (amount - 1) // 2
    giver, sink = sizes[1:1 + 2 * twos:2], sizes[2:2 + 2 * twos:2]
    margin = jnp.minimum(giver - 1, most - sink)
    moved = jax.random.randint(jax.random.fold_in(stream_key, 1), (twos,), 0, 1 << 20) % (margin + 1)
    sizes = sizes.at[1:1 + 2 * twos:2].set(giver - moved).at[2:2 + 2 * twos:2].set(sink + moved)
    return sizes[jax.random.permutation(jax.random.fold_in(stream_key, 2), amount)]


def assign_block(key, own, number, rows, amount, top, reach, slope):
    order = jax.random.permutation(key, amount)
    crowded, ordinary = load_shares(amount, rows * top, reach, slope, True), load_shares(amount, rows * top, reach, slope, False)
    places = jnp.arange(amount)

    def named(lengths, offset_by):
        used = int((lengths > 0).sum())
        fixed = max(1, used // 4)
        passed = fixed + (places - fixed + offset_by * (used - fixed)) % max(1, amount - fixed)
        return jnp.zeros((amount,), jnp.int32).at[order[jnp.where(places < fixed, places, passed)]].set(jnp.asarray(lengths, jnp.int32))

    lengths = jnp.where(number % 4 == 0, named(crowded, number // 4), named(ordinary, number - number // 4 - 1))
    mixed = jax.random.permutation(jax.random.fold_in(own, 3), amount)
    source_of, receiver = mixed[0:amount // 2 * 2:2], mixed[1:amount // 2 * 2:2]
    margin = jnp.minimum(lengths[source_of] - 1, reach - lengths[receiver]) // 2
    margin = jnp.where((source_of == order[0]) | (receiver == order[0]) | (lengths[receiver] == 0), 0, jnp.maximum(margin, 0))
    passed = jax.random.randint(jax.random.fold_in(own, 4), (amount // 2,), 0, 1 << 20) % (margin + 1)
    lengths = lengths.at[source_of].add(-passed).at[receiver].add(passed)
    labels = jnp.searchsorted(jnp.cumsum(lengths), jnp.arange(rows * top), side="right").astype(jnp.int32)
    grid = labels.reshape(top, rows).T
    grid = grid[jax.random.permutation(jax.random.fold_in(own, 1), rows)]
    offset_by = jax.random.randint(jax.random.fold_in(own, 2), (rows, 1), 0, top)
    return jnp.take_along_axis(grid, (jnp.arange(top)[None, :] + offset_by) % top, axis=1)


def load_shares(number_of, total, bound, skew, full):
    weights = [(1 << 20) // math.isqrt(rank ** skew) + 1 for rank in range(1, number_of + 1)]
    largest = bound if full else min(bound, max(-(-total // number_of), total * weights[0] // sum(weights)))
    least = 1 if total - largest >= number_of - 1 else 0
    holding, rest = [largest] + [least] * (number_of - 1), total - largest - least * (number_of - 1)
    while rest > 0:
        movable = [i for i in range(1, number_of) if holding[i] < largest] or [i for i in range(1, number_of) if holding[i] < bound]
        whole, budget = sum([weights[i] for i in movable]), rest
        for i in movable:
            addition = min(bound - holding[i], max(1, budget * weights[i] // whole), rest)
            holding[i] = holding[i] + addition
            rest = rest - addition
    return np.array(holding)


def scatter_about(rng, extent, spread, bound, pieces=(), kind=jnp.bfloat16):
    drawn = jax.random.normal(rng, extent, jnp.float32) * spread
    if len(pieces) > 0:
        drawn = shard_levels(rng, extent, pieces, -0.22, 0.18) * drawn
    return jnp.clip(drawn, min=-bound, max=bound).astype(kind)


def setup_inputs(seed: int = 0) -> dict:
    key_of = jax.random.split(jax.random.key(seed), 14)
    hidden = draw_hidden(jax.random.fold_in(key_of[13], 71), 0)
    segment_ids = jnp.searchsorted(jnp.cumsum(uneven_parts(key_of[1], SEGS, TOKENS, SEG_MAX, 2)), jnp.arange(TOKENS), side="right").astype(jnp.int32)
    routes_keys = jax.random.split(jax.random.fold_in(key_of[2], 1), TOKENS // (TOK_DEV // COPIES))
    routes_turns = jax.random.permutation(jax.random.fold_in(key_of[2], 3), TOKENS // (TOK_DEV // COPIES))
    routes = jax.vmap(lambda own, number: assign_block(jax.random.fold_in(key_of[2], 2), own, number, TOK_DEV // COPIES, EXPERTS, TOPK, CAP, 1))(routes_keys, routes_turns).reshape((TOKENS, TOPK))
    gates = jnp.clip(0.02 + 0.23 * jax.random.uniform(key_of[3], (TOKENS, TOPK), jnp.float32) ** shard_levels(key_of[3], (TOKENS, TOPK), ((0, 8),), -0.2, 0.2), 0.02, 0.25)
    norm_attn = jnp.clip(1.0 + 0.1 * jax.random.normal(key_of[4], (D,), jnp.float32), 0.5, 1.5).astype(jnp.bfloat16)
    norm_moe = jnp.clip(1.0 + 0.1 * jax.random.normal(key_of[5], (D,), jnp.float32), 0.5, 1.5).astype(jnp.bfloat16)
    w_query = draw_w_query(jax.random.fold_in(key_of[13], 71), 0)
    w_key = draw_w_key(jax.random.fold_in(key_of[13], 71), 0)
    w_value = scatter_about(key_of[8], (D, KV_HEADS * HEAD_DIM), D ** -0.5, 0.1875, ((1, 4),))
    w_out = scatter_about(key_of[9], (HEADS * HEAD_DIM, D), (HEAD_DIM // 2) ** -0.5, 1.0, ((0, 4),))
    w_gate = draw_w_gate(jax.random.fold_in(key_of[13], 71), 0)
    w_up = draw_w_up(jax.random.fold_in(key_of[13], 71), 0)
    w_down = draw_w_down(jax.random.fold_in(key_of[13], 71), 0)
    return {"hidden": hidden, "segment_ids": segment_ids, "routes": routes, "gates": gates, "norm_attn": norm_attn, "norm_moe": norm_moe, "w_query": w_query, "w_key": w_key, "w_value": w_value, "w_out": w_out, "w_gate": w_gate, "w_up": w_up, "w_down": w_down}


EPS = 1e-06
SCORE_SCALE = 0.015625

def normalize(values, gain):
    widened = values.astype(jnp.float32)
    return widened * lax.rsqrt(lax.optimization_barrier(jnp.mean(widened * widened, axis=-1, keepdims=True)) + EPS) * gain.astype(jnp.float32)

def rotary(tensor, positions):
    half_dim = tensor.shape[-1] // 2
    frequencies = 10000.0 ** (-jnp.arange(half_dim, dtype=jnp.float32) * 2.0 / tensor.shape[-1])
    angles = positions.astype(jnp.float32)[:, None] * frequencies[None, :]
    cosine = jnp.cos(angles)[:, None, :]
    sine_part = jnp.sin(angles)[:, None, :]
    lower_half = tensor[..., :half_dim]
    upper_half = tensor[..., half_dim:]
    return jnp.concatenate([lower_half * cosine - upper_half * sine_part, upper_half * cosine + lower_half * sine_part], axis=-1)

def segment_positions(segment_ids):
    index_all = jnp.arange(segment_ids.shape[0], dtype=jnp.int32)
    changed = jnp.concatenate([jnp.ones((1,), jnp.bool_), segment_ids[1:] != segment_ids[:-1]])
    starts = lax.cummax(jnp.where(changed, index_all, 0), axis=0)
    return index_all - starts

def attention(queries, key_rot, value_heads, segment_ids):
    total_rows = queries.shape[0]
    block_rows = min(512, total_rows)
    group_size = HEADS // KV_HEADS
    block_count = total_rows // block_rows
    grouped = queries.reshape(block_count, block_rows, KV_HEADS, group_size, HEAD_DIM)

    def one_block(query_block):
        query_rows = lax.dynamic_index_in_dim(grouped, query_block, 0, keepdims=False).astype(jnp.float32)
        query_start = query_block * block_rows
        query_index = query_start + jnp.arange(block_rows, dtype=jnp.int32)
        query_segs = lax.dynamic_slice_in_dim(segment_ids, query_start, block_rows)

        def visit_block(key_block, carried):
            key_start = key_block * block_rows
            key_segs = lax.dynamic_slice_in_dim(segment_ids, key_start, block_rows)

            def update(state):
                running_max, weight_sum, accumulated = state
                key_rows = lax.dynamic_slice_in_dim(key_rot, key_start, block_rows).astype(jnp.float32)
                value_rows = lax.dynamic_slice_in_dim(value_heads, key_start, block_rows).astype(jnp.float32)
                scores = jnp.einsum('tkgd,skd->kgts', query_rows, key_rows) * SCORE_SCALE
                key_index = key_start + jnp.arange(block_rows, dtype=jnp.int32)
                allowed = (query_segs[:, None] == key_segs[None, :]) & (query_index[:, None] >= key_index[None, :])
                masked = jnp.where(allowed, scores, -1e+30)
                new_max = jnp.maximum(running_max, lax.optimization_barrier(jnp.max(masked, axis=-1)))
                weights = jnp.where(allowed, jnp.exp(masked - new_max[..., None]), 0.0)
                factor = jnp.exp(running_max - new_max)
                weight_sum = weight_sum * factor + lax.optimization_barrier(jnp.sum(weights, axis=-1))
                rounded = lax.optimization_barrier(weights.astype(jnp.bfloat16)).astype(jnp.float32)
                accumulated = accumulated * factor[..., None] + jnp.einsum('kgts,skd->kgtd', rounded, value_rows)
                return (new_max, weight_sum, accumulated)
            relevant = key_segs[block_rows - 1] >= query_segs[0]
            return lax.cond(relevant, update, lambda state: state, carried)
        start_state = (jnp.full((KV_HEADS, group_size, block_rows), -1e+30, jnp.float32), jnp.zeros((KV_HEADS, group_size, block_rows), jnp.float32), jnp.zeros((KV_HEADS, group_size, block_rows, HEAD_DIM), jnp.float32))
        running_max, weight_sum, accumulated = lax.fori_loop(0, query_block + 1, visit_block, start_state)
        result = accumulated / weight_sum[..., None]
        return result.transpose(2, 0, 1, 3).reshape(block_rows, HEADS * HEAD_DIM).astype(jnp.bfloat16)
    blocks = lax.map(one_block, jnp.arange(block_count, dtype=jnp.int32))
    return blocks.reshape(total_rows, HEADS * HEAD_DIM)

def experts_reference(normed_rows, routes, gates, w_gate, w_up, w_down):
    total_rows, route_count = routes.shape
    flat = routes.reshape(-1)
    items = flat.shape[0]
    tile_rows = 256
    order = jnp.argsort(flat, stable=True).astype(jnp.int32)
    sorted_experts = flat[order]
    counts = lax.optimization_barrier(jnp.sum((flat[:, None] == jnp.arange(EXPERTS, dtype=jnp.int32)[None, :]).astype(jnp.int32), axis=0))
    padded_counts = (counts + tile_rows - 1) // tile_rows * tile_rows
    pad_starts = jnp.cumsum(padded_counts) - padded_counts
    plain_starts = jnp.cumsum(counts) - counts
    slot_index = pad_starts[sorted_experts] + jnp.arange(items, dtype=jnp.int32) - plain_starts[sorted_experts]
    tile_total = (items + tile_rows - 1) // tile_rows + EXPERTS
    capacity_rows = tile_total * tile_rows
    token_of = jnp.full((capacity_rows,), total_rows, jnp.int32).at[slot_index].set((order // route_count).astype(jnp.int32))
    gate_of = jnp.zeros((capacity_rows,), jnp.float32).at[slot_index].set(gates.reshape(-1)[order])
    tile_starts = jnp.arange(tile_total, dtype=jnp.int32) * tile_rows
    tile_expert = lax.optimization_barrier(jnp.sum((pad_starts[None, :] <= tile_starts[:, None]).astype(jnp.int32), axis=1)) - 1
    padded_rows = jnp.concatenate([normed_rows, jnp.zeros((1, normed_rows.shape[1]), normed_rows.dtype)])
    group_units = FF // N_TP

    def tile_step(accumulated, tile):
        rows_index = lax.dynamic_slice_in_dim(token_of, tile * tile_rows, tile_rows)
        tile_gates = lax.dynamic_slice_in_dim(gate_of, tile * tile_rows, tile_rows)
        expert = tile_expert[tile]
        rows = padded_rows[rows_index].astype(jnp.float32)
        gate_val = jnp.dot(rows, w_gate[expert].astype(jnp.float32))
        up_val = jnp.dot(rows, w_up[expert].astype(jnp.float32))
        activated = lax.optimization_barrier((jax.nn.silu(gate_val) * up_val).astype(jnp.bfloat16)).astype(jnp.float32)
        split_act = activated.reshape(tile_rows, N_TP, group_units)
        split_down = w_down[expert].astype(jnp.float32).reshape(N_TP, group_units, D)
        partial_value = jnp.einsum('tqf,qfd->tqd', split_act, split_down).astype(jnp.bfloat16)
        partial_value = lax.optimization_barrier(partial_value).astype(jnp.float32)
        output_rows = lax.optimization_barrier(jnp.sum(partial_value, axis=1)) * tile_gates[:, None]
        return (accumulated.at[rows_index].add(output_rows), None)
    start_sum = jnp.zeros((total_rows + 1, normed_rows.shape[1]), jnp.float32)
    result, unused = lax.scan(tile_step, start_sum, jnp.arange(tile_total, dtype=jnp.int32))
    return result[:total_rows]

def reference(hidden, segment_ids, routes, gates, norm_attn, norm_moe, w_query, w_key, w_value, w_out, w_gate, w_up, w_down):
    positions = segment_positions(segment_ids)
    normed = normalize(hidden, norm_attn).astype(jnp.bfloat16)
    queries = jnp.dot(normed, w_query, preferred_element_type=jnp.float32).reshape(TOKENS, HEADS, HEAD_DIM)
    queries = rotary(queries, positions).astype(jnp.bfloat16)
    key_raw = jnp.dot(normed, w_key, preferred_element_type=jnp.float32).reshape(TOKENS, KV_HEADS, HEAD_DIM)
    value_proj = jnp.dot(normed, w_value, preferred_element_type=jnp.float32).astype(jnp.bfloat16)
    kv_cache = jnp.stack([key_raw.reshape(TOKENS, KV_HEADS * HEAD_DIM).astype(jnp.bfloat16), value_proj], axis=1)
    key_rot = rotary(key_raw, positions).astype(jnp.bfloat16)
    value_heads = value_proj.reshape(TOKENS, KV_HEADS, HEAD_DIM)
    attended = attention(queries, key_rot, value_heads, segment_ids)
    mixed = jnp.dot(attended, w_out, preferred_element_type=jnp.float32)
    residual = (hidden.astype(jnp.float32) + mixed).astype(jnp.bfloat16)
    normed_moe = normalize(residual, norm_moe).astype(jnp.bfloat16)
    expert_sum = experts_reference(normed_moe, routes, gates, w_gate, w_up, w_down)
    hidden_out = (residual.astype(jnp.float32) + expert_sum).astype(jnp.bfloat16)
    return (hidden_out, kv_cache)
```

```python
import jax
import jax.numpy as jnp
from jax import lax
from jax.sharding import PartitionSpec as P

HEAD_DIM = 64
EXPERTS = 32


EPS = 1e-06
SCORE_SCALE = 0.015625


def normalize(values, gain):
    widened = values.astype(jnp.float32)
    return (
        widened
        * lax.rsqrt(jnp.mean(widened * widened, axis=-1, keepdims=True) + EPS)
        * gain.astype(jnp.float32)
    )


def rotary(tensor, positions):
    half_dim = tensor.shape[-1] // 2
    frequencies = 10000.0 ** (-jnp.arange(half_dim, dtype=jnp.float32) * 2.0 / tensor.shape[-1])
    angles = positions.astype(jnp.float32)[:, None] * frequencies[None, :]
    cosine = jnp.cos(angles)[:, None, :]
    sine_part = jnp.sin(angles)[:, None, :]
    lower_half = tensor[..., :half_dim]
    upper_half = tensor[..., half_dim:]
    return jnp.concatenate(
        [
            lower_half * cosine - upper_half * sine_part,
            upper_half * cosine + lower_half * sine_part,
        ],
        axis=-1,
    )


def segment_positions(segment_ids):
    index_all = jnp.arange(segment_ids.shape[0], dtype=jnp.int32)
    changed = jnp.concatenate([jnp.ones((1,), jnp.bool_), segment_ids[1:] != segment_ids[:-1]])
    starts = lax.cummax(jnp.where(changed, index_all, 0), axis=0)
    return index_all - starts


def per_device_routed(
    hidden,
    segment_ids,
    routes,
    gates,
    norm_attn,
    norm_moe,
    w_query,
    w_key,
    w_value,
    w_out,
    w_gate,
    w_up,
    w_down,
):
    tokens = hidden.shape[0]
    model_width = hidden.shape[1]
    first_row = lax.axis_index("seq") * tokens
    positions = lax.dynamic_slice_in_dim(segment_positions(segment_ids), first_row, tokens)
    own_segs = lax.dynamic_slice_in_dim(segment_ids, first_row, tokens)
    normed = normalize(hidden, norm_attn).astype(jnp.bfloat16)
    query_heads = w_query.shape[1] // HEAD_DIM
    kv_heads = w_key.shape[1] // HEAD_DIM
    group_size = query_heads // kv_heads
    queries = jnp.dot(normed, w_query, preferred_element_type=jnp.float32).reshape(
        tokens, query_heads, HEAD_DIM
    )
    queries = (
        rotary(queries, positions)
        .astype(jnp.bfloat16)
        .reshape(tokens, kv_heads, group_size, HEAD_DIM)
    )
    key_raw = jnp.dot(normed, w_key, preferred_element_type=jnp.float32).reshape(
        tokens, kv_heads, HEAD_DIM
    )
    value_proj = jnp.dot(normed, w_value, preferred_element_type=jnp.float32).astype(jnp.bfloat16)
    kv_cache = jnp.stack(
        [key_raw.reshape(tokens, kv_heads * HEAD_DIM).astype(jnp.bfloat16), value_proj], axis=1
    )
    key_rot = rotary(key_raw, positions).astype(jnp.bfloat16)
    value_heads = value_proj.reshape(tokens, kv_heads, HEAD_DIM)
    query_index = first_row + jnp.arange(tokens, dtype=jnp.int32)
    last_query = first_row + tokens - 1
    lowest_seg = own_segs[0]

    def attend(carried, key_rows, value_rows, key_start, key_segs):
        running_max, weight_sum, accumulated = carried
        scores = (
            jnp.einsum("tkgd,skd->kgts", queries, key_rows, preferred_element_type=jnp.float32)
            * SCORE_SCALE
        )
        key_index = key_start + jnp.arange(key_rows.shape[0], dtype=jnp.int32)
        allowed = (own_segs[:, None] == key_segs[None, :]) & (
            query_index[:, None] >= key_index[None, :]
        )
        masked = jnp.where(allowed, scores, -1e30)
        new_max = jnp.maximum(running_max, jnp.max(masked, axis=-1))
        weights = jnp.where(allowed, jnp.exp(masked - new_max[..., None]), 0.0)
        factor = jnp.exp(running_max - new_max)
        weight_sum = weight_sum * factor + jnp.sum(weights, axis=-1)
        accumulated = accumulated * factor[..., None] + jnp.einsum(
            "kgts,skd->kgtd",
            weights.astype(jnp.bfloat16),
            value_rows,
            preferred_element_type=jnp.float32,
        )
        return (new_max, weight_sum, accumulated)

    start_state = (
        jnp.full((kv_heads, group_size, tokens), -1e30, jnp.float32),
        jnp.zeros((kv_heads, group_size, tokens), jnp.float32),
        jnp.zeros((kv_heads, group_size, tokens, HEAD_DIM), jnp.float32),
    )
    keys_all = lax.all_gather(key_rot, "seq", axis=0, tiled=True)
    values_all = lax.all_gather(value_heads, "seq", axis=0, tiled=True)
    block_total = keys_all.shape[0] // tokens

    def visit_block(block_index, state_now):
        key_start = block_index * tokens
        key_rows = lax.dynamic_slice_in_dim(keys_all, block_index * tokens, tokens)
        value_rows = lax.dynamic_slice_in_dim(values_all, block_index * tokens, tokens)
        key_segs = lax.dynamic_slice_in_dim(segment_ids, key_start, tokens)
        relevant = (key_start <= last_query) & (key_segs[tokens - 1] >= lowest_seg)
        return lax.cond(
            relevant,
            lambda inner: attend(inner, key_rows, value_rows, key_start, key_segs),
            lambda inner: inner,
            state_now,
        )

    running_max, weight_sum, accumulated = lax.fori_loop(0, block_total, visit_block, start_state)
    attended = (
        (accumulated / weight_sum[..., None])
        .transpose(2, 0, 1, 3)
        .reshape(tokens, query_heads * HEAD_DIM)
    )
    attended = attended.astype(jnp.bfloat16)
    partial_out = jnp.dot(attended, w_out, preferred_element_type=jnp.float32)
    attn_mixed = lax.psum(partial_out.astype(jnp.bfloat16), "tp").astype(jnp.float32)
    residual = (hidden.astype(jnp.float32) + attn_mixed).astype(jnp.bfloat16)
    normed_moe = normalize(residual, norm_moe).astype(jnp.bfloat16)
    route_count = routes.shape[1]
    slots_dev = w_gate.shape[0]
    seq_count = lax.axis_size("seq")
    slot_total = slots_dev * seq_count
    copies = slot_total // EXPERTS
    block_rows = tokens // copies
    capacity = 2 * block_rows * route_count // EXPERTS
    copy_of = (jnp.arange(tokens, dtype=jnp.int32) // block_rows)[:, None]
    slot_of = routes + EXPERTS * copy_of
    flat_expert = routes.reshape(copies, block_rows * route_count)
    onehot = (
        flat_expert[:, :, None] == jnp.arange(EXPERTS, dtype=jnp.int32)[None, None, :]
    ).astype(jnp.int32)
    before = jnp.cumsum(onehot, axis=1) - onehot
    slot_rank = jnp.sum(before * onehot, axis=2).reshape(tokens, route_count)
    target = slot_of * capacity + slot_rank
    token_ids = jnp.broadcast_to(
        jnp.arange(tokens, dtype=jnp.int32)[:, None], (tokens, route_count)
    )
    source = (
        jnp.full((slot_total * capacity,), tokens, jnp.int32)
        .at[target.reshape(-1)]
        .set(token_ids.reshape(-1))
    )
    padded_rows = jnp.concatenate([normed_moe, jnp.zeros((1, normed_moe.shape[1]), jnp.bfloat16)])
    outbound = padded_rows[source].reshape(seq_count, slots_dev, capacity, normed_moe.shape[1])
    arrived = lax.all_to_all(outbound, "seq", split_axis=0, concat_axis=0, tiled=True)
    gate_val = jnp.einsum("jsrd,sdf->jsrf", arrived, w_gate, preferred_element_type=jnp.float32)
    up_val = jnp.einsum("jsrd,sdf->jsrf", arrived, w_up, preferred_element_type=jnp.float32)
    activated = (jax.nn.silu(gate_val) * up_val).astype(jnp.bfloat16)
    group_part = jnp.einsum("jsrf,sfd->jsrd", activated, w_down, preferred_element_type=jnp.float32)
    result = group_part.astype(jnp.bfloat16)
    returned = lax.all_to_all(result, "seq", split_axis=0, concat_axis=0, tiled=True).reshape(
        slot_total * capacity, model_width
    )
    picked = returned[target]
    combined = jnp.einsum(
        "tk,tkd->td",
        gates,
        picked,
        preferred_element_type=jnp.float32,
        precision=lax.Precision.HIGHEST,
    )
    expert_sum = lax.psum(combined.astype(jnp.bfloat16), "tp").astype(jnp.float32)
    hidden_out = (residual.astype(jnp.float32) + expert_sum).astype(jnp.bfloat16)
    return (hidden_out, kv_cache)


def attention_inputs(hidden, segment_ids, norm_attn, w_query, w_key, w_value):
    tokens = hidden.shape[0]
    first_row = lax.axis_index("seq") * tokens
    own_segs = lax.dynamic_slice_in_dim(segment_ids, first_row, tokens)
    query_index = first_row + jnp.arange(tokens, dtype=jnp.int32)
    starts = jnp.sum((segment_ids[None, :] < own_segs[:, None]).astype(jnp.int32), axis=1)
    positions = query_index - starts
    normed = normalize(hidden, norm_attn).astype(jnp.bfloat16)
    query_heads = w_query.shape[1] // HEAD_DIM
    kv_heads = w_key.shape[1] // HEAD_DIM
    queries = jnp.dot(normed, w_query, preferred_element_type=jnp.float32)
    key_raw = jnp.dot(normed, w_key, preferred_element_type=jnp.float32)
    value_proj = jnp.dot(normed, w_value, preferred_element_type=jnp.float32).astype(jnp.bfloat16)
    kv_cache = jnp.stack([key_raw.astype(jnp.bfloat16), value_proj], axis=1)
    queries = rotary(queries.reshape(tokens, query_heads, HEAD_DIM), positions)
    key_rot = rotary(key_raw.reshape(tokens, kv_heads, HEAD_DIM), positions)
    queries = queries.astype(jnp.bfloat16)
    key_rot = key_rot.astype(jnp.bfloat16).reshape(tokens, kv_heads * HEAD_DIM)
    return queries, key_rot, value_proj, kv_cache, own_segs, query_index, starts


def attend_all(queries, keys_all, values_all, query_index, starts):
    tokens, query_heads, _ = queries.shape
    total = keys_all.shape[0]
    kv_heads = keys_all.shape[1] // HEAD_DIM
    grouped = queries.reshape(tokens, kv_heads, query_heads // kv_heads, HEAD_DIM)
    keys = keys_all.reshape(total, kv_heads, HEAD_DIM)
    values = values_all.reshape(total, kv_heads, HEAD_DIM)
    scores = (
        jnp.einsum("tkgd,skd->kgts", grouped, keys, preferred_element_type=jnp.float32)
        * SCORE_SCALE
    )
    key_index = jnp.arange(total, dtype=jnp.int32)
    allowed = (key_index[None, :] <= query_index[:, None]) & (
        key_index[None, :] >= starts[:, None]
    )
    masked = jnp.where(allowed, scores, -1e30)
    top = jnp.max(masked, axis=-1, keepdims=True)
    weights = jnp.where(allowed, jnp.exp(masked - top), 0.0)
    weight_sum = jnp.sum(weights, axis=-1)
    mixed = jnp.einsum(
        "kgts,skd->kgtd",
        weights.astype(jnp.bfloat16),
        values,
        preferred_element_type=jnp.float32,
    )
    attended = (mixed / weight_sum[..., None]).transpose(2, 0, 1, 3)
    return attended.reshape(tokens, query_heads * HEAD_DIM).astype(jnp.bfloat16)


def expert_gates(routes, gates, experts):
    hit = routes[:, :, None] == jnp.arange(experts, dtype=jnp.int32)[None, None, :]
    return jnp.sum(jnp.where(hit, gates[:, :, None], 0.0), axis=1)


def per_device(
    hidden,
    segment_ids,
    routes,
    gates,
    norm_attn,
    norm_moe,
    w_query,
    w_key,
    w_value,
    w_out,
    w_gate,
    w_up,
    w_down,
):
    tokens, width = hidden.shape
    slots, _, units = w_gate.shape
    part = tokens // lax.axis_size("tp")
    queries, key_rot, value_proj, kv_cache, own_segs, query_index, starts = attention_inputs(
        hidden, segment_ids, norm_attn, w_query, w_key, w_value
    )
    table = lax.all_gather(expert_gates(routes, gates, EXPERTS), "seq", axis=0, tiled=True)
    own_gates = lax.dynamic_slice_in_dim(table, lax.axis_index("seq") * slots, slots, axis=1)
    kv = lax.all_gather(
        jnp.concatenate([key_rot, value_proj], axis=1), "seq", axis=0, tiled=True
    )
    half = kv.shape[1] // 2
    attended = attend_all(queries, kv[:, :half], kv[:, half:], query_index, starts)
    partial_out = jnp.dot(attended, w_out, preferred_element_type=jnp.float32)
    mixed = lax.psum_scatter(
        partial_out.astype(jnp.bfloat16), "tp", scatter_dimension=0, tiled=True
    )
    own_part = lax.dynamic_slice_in_dim(hidden, lax.axis_index("tp") * part, part)
    residual = (own_part.astype(jnp.float32) + mixed.astype(jnp.float32)).astype(jnp.bfloat16)
    normed = normalize(residual, norm_moe).astype(jnp.bfloat16)
    rows = lax.all_gather(normed, ("seq", "tp"), axis=0, tiled=True)
    total = jnp.zeros((rows.shape[0], width), jnp.float32)
    for slot in range(slots):
        gate_val = jnp.dot(rows, w_gate[slot], preferred_element_type=jnp.float32)
        up_val = jnp.dot(rows, w_up[slot], preferred_element_type=jnp.float32)
        scale = own_gates[:, slot : slot + 1]
        act = jnp.where(scale > 0, jax.nn.silu(gate_val) * up_val * scale, 0.0)
        total = total + jnp.dot(
            act.astype(jnp.bfloat16), w_down[slot], preferred_element_type=jnp.float32
        )
    summed = lax.psum_scatter(
        total.astype(jnp.bfloat16), ("seq", "tp"), scatter_dimension=0, tiled=True
    )
    out_part = (residual.astype(jnp.float32) + summed.astype(jnp.float32)).astype(jnp.bfloat16)
    return lax.all_gather(out_part, "tp", axis=0, tiled=True), kv_cache


def solution(mesh):
    whole_rows = mesh.shape["seq"] <= 8
    return jax.shard_map(
        per_device if whole_rows else per_device_routed,
        mesh=mesh,
        in_specs=(
            P("seq", None),
            P(),
            P("seq", None),
            P("seq", None),
            P(),
            P(),
            P(None, "tp"),
            P(None, "tp"),
            P(None, "tp"),
            P("tp", None),
            P("seq", None, "tp"),
            P("seq", None, "tp"),
            P("seq", "tp", None),
        ),
        out_specs=(P("seq", None), P("seq", None, "tp")),
        check_vma=False,
    )
```

```python
import jax
import jax.numpy as jnp
from jax import lax
from jax.experimental import pallas as pl
from jax.experimental.pallas import tpu as pltpu
from jax.sharding import PartitionSpec as P

HEAD_DIM = 64
EXPERTS = 32


EPS = 1e-06
SCORE_SCALE = 0.015625


def normalize(values, gain):
    widened = values.astype(jnp.float32)
    return (
        widened
        * lax.rsqrt(jnp.mean(widened * widened, axis=-1, keepdims=True) + EPS)
        * gain.astype(jnp.float32)
    )


def rotary(tensor, positions):
    half_dim = tensor.shape[-1] // 2
    frequencies = 10000.0 ** (-jnp.arange(half_dim, dtype=jnp.float32) * 2.0 / tensor.shape[-1])
    angles = positions.astype(jnp.float32)[:, None] * frequencies[None, :]
    cosine = jnp.cos(angles)[:, None, :]
    sine_part = jnp.sin(angles)[:, None, :]
    lower_half = tensor[..., :half_dim]
    upper_half = tensor[..., half_dim:]
    return jnp.concatenate(
        [
            lower_half * cosine - upper_half * sine_part,
            upper_half * cosine + lower_half * sine_part,
        ],
        axis=-1,
    )


def segment_positions(segment_ids):
    index_all = jnp.arange(segment_ids.shape[0], dtype=jnp.int32)
    changed = jnp.concatenate([jnp.ones((1,), jnp.bool_), segment_ids[1:] != segment_ids[:-1]])
    starts = lax.cummax(jnp.where(changed, index_all, 0), axis=0)
    return index_all - starts


def per_device_routed(
    hidden,
    segment_ids,
    routes,
    gates,
    norm_attn,
    norm_moe,
    w_query,
    w_key,
    w_value,
    w_out,
    w_gate,
    w_up,
    w_down,
):
    tokens = hidden.shape[0]
    model_width = hidden.shape[1]
    first_row = lax.axis_index("seq") * tokens
    positions = lax.dynamic_slice_in_dim(segment_positions(segment_ids), first_row, tokens)
    own_segs = lax.dynamic_slice_in_dim(segment_ids, first_row, tokens)
    normed = normalize(hidden, norm_attn).astype(jnp.bfloat16)
    query_heads = w_query.shape[1] // HEAD_DIM
    kv_heads = w_key.shape[1] // HEAD_DIM
    group_size = query_heads // kv_heads
    queries = jnp.dot(normed, w_query, preferred_element_type=jnp.float32).reshape(
        tokens, query_heads, HEAD_DIM
    )
    queries = (
        rotary(queries, positions)
        .astype(jnp.bfloat16)
        .reshape(tokens, kv_heads, group_size, HEAD_DIM)
    )
    key_raw = jnp.dot(normed, w_key, preferred_element_type=jnp.float32).reshape(
        tokens, kv_heads, HEAD_DIM
    )
    value_proj = jnp.dot(normed, w_value, preferred_element_type=jnp.float32).astype(jnp.bfloat16)
    kv_cache = jnp.stack(
        [key_raw.reshape(tokens, kv_heads * HEAD_DIM).astype(jnp.bfloat16), value_proj], axis=1
    )
    key_rot = rotary(key_raw, positions).astype(jnp.bfloat16)
    value_heads = value_proj.reshape(tokens, kv_heads, HEAD_DIM)
    query_index = first_row + jnp.arange(tokens, dtype=jnp.int32)
    last_query = first_row + tokens - 1
    lowest_seg = own_segs[0]

    def attend(carried, key_rows, value_rows, key_start, key_segs):
        running_max, weight_sum, accumulated = carried
        scores = (
            jnp.einsum("tkgd,skd->kgts", queries, key_rows, preferred_element_type=jnp.float32)
            * SCORE_SCALE
        )
        key_index = key_start + jnp.arange(key_rows.shape[0], dtype=jnp.int32)
        allowed = (own_segs[:, None] == key_segs[None, :]) & (
            query_index[:, None] >= key_index[None, :]
        )
        masked = jnp.where(allowed, scores, -1e30)
        new_max = jnp.maximum(running_max, jnp.max(masked, axis=-1))
        weights = jnp.where(allowed, jnp.exp(masked - new_max[..., None]), 0.0)
        factor = jnp.exp(running_max - new_max)
        weight_sum = weight_sum * factor + jnp.sum(weights, axis=-1)
        accumulated = accumulated * factor[..., None] + jnp.einsum(
            "kgts,skd->kgtd",
            weights.astype(jnp.bfloat16),
            value_rows,
            preferred_element_type=jnp.float32,
        )
        return (new_max, weight_sum, accumulated)

    start_state = (
        jnp.full((kv_heads, group_size, tokens), -1e30, jnp.float32),
        jnp.zeros((kv_heads, group_size, tokens), jnp.float32),
        jnp.zeros((kv_heads, group_size, tokens, HEAD_DIM), jnp.float32),
    )
    keys_all = lax.all_gather(key_rot, "seq", axis=0, tiled=True)
    values_all = lax.all_gather(value_heads, "seq", axis=0, tiled=True)
    block_total = keys_all.shape[0] // tokens

    def visit_block(block_index, state_now):
        key_start = block_index * tokens
        key_rows = lax.dynamic_slice_in_dim(keys_all, block_index * tokens, tokens)
        value_rows = lax.dynamic_slice_in_dim(values_all, block_index * tokens, tokens)
        key_segs = lax.dynamic_slice_in_dim(segment_ids, key_start, tokens)
        relevant = (key_start <= last_query) & (key_segs[tokens - 1] >= lowest_seg)
        return lax.cond(
            relevant,
            lambda inner: attend(inner, key_rows, value_rows, key_start, key_segs),
            lambda inner: inner,
            state_now,
        )

    running_max, weight_sum, accumulated = lax.fori_loop(0, block_total, visit_block, start_state)
    attended = (
        (accumulated / weight_sum[..., None])
        .transpose(2, 0, 1, 3)
        .reshape(tokens, query_heads * HEAD_DIM)
    )
    attended = attended.astype(jnp.bfloat16)
    partial_out = jnp.dot(attended, w_out, preferred_element_type=jnp.float32)
    attn_mixed = lax.psum(partial_out.astype(jnp.bfloat16), "tp").astype(jnp.float32)
    residual = (hidden.astype(jnp.float32) + attn_mixed).astype(jnp.bfloat16)
    normed_moe = normalize(residual, norm_moe).astype(jnp.bfloat16)
    route_count = routes.shape[1]
    slots_dev = w_gate.shape[0]
    seq_count = lax.axis_size("seq")
    slot_total = slots_dev * seq_count
    copies = slot_total // EXPERTS
    block_rows = tokens // copies
    capacity = 2 * block_rows * route_count // EXPERTS
    copy_of = (jnp.arange(tokens, dtype=jnp.int32) // block_rows)[:, None]
    slot_of = routes + EXPERTS * copy_of
    flat_expert = routes.reshape(copies, block_rows * route_count)
    onehot = (
        flat_expert[:, :, None] == jnp.arange(EXPERTS, dtype=jnp.int32)[None, None, :]
    ).astype(jnp.int32)
    before = jnp.cumsum(onehot, axis=1) - onehot
    slot_rank = jnp.sum(before * onehot, axis=2).reshape(tokens, route_count)
    target = slot_of * capacity + slot_rank
    token_ids = jnp.broadcast_to(
        jnp.arange(tokens, dtype=jnp.int32)[:, None], (tokens, route_count)
    )
    source = (
        jnp.full((slot_total * capacity,), tokens, jnp.int32)
        .at[target.reshape(-1)]
        .set(token_ids.reshape(-1))
    )
    padded_rows = jnp.concatenate([normed_moe, jnp.zeros((1, normed_moe.shape[1]), jnp.bfloat16)])
    outbound = padded_rows[source].reshape(seq_count, slots_dev, capacity, normed_moe.shape[1])
    arrived = lax.all_to_all(outbound, "seq", split_axis=0, concat_axis=0, tiled=True)
    gate_val = jnp.einsum("jsrd,sdf->jsrf", arrived, w_gate, preferred_element_type=jnp.float32)
    up_val = jnp.einsum("jsrd,sdf->jsrf", arrived, w_up, preferred_element_type=jnp.float32)
    activated = (jax.nn.silu(gate_val) * up_val).astype(jnp.bfloat16)
    group_part = jnp.einsum("jsrf,sfd->jsrd", activated, w_down, preferred_element_type=jnp.float32)
    result = group_part.astype(jnp.bfloat16)
    returned = lax.all_to_all(result, "seq", split_axis=0, concat_axis=0, tiled=True).reshape(
        slot_total * capacity, model_width
    )
    picked = returned[target]
    combined = jnp.einsum(
        "tk,tkd->td",
        gates,
        picked,
        preferred_element_type=jnp.float32,
        precision=lax.Precision.HIGHEST,
    )
    expert_sum = lax.psum(combined.astype(jnp.bfloat16), "tp").astype(jnp.float32)
    hidden_out = (residual.astype(jnp.float32) + expert_sum).astype(jnp.bfloat16)
    return (hidden_out, kv_cache)


def attention_inputs(hidden, segment_ids, norm_attn, w_query, w_key, w_value):
    tokens = hidden.shape[0]
    first_row = lax.axis_index("seq") * tokens
    own_segs = lax.dynamic_slice_in_dim(segment_ids, first_row, tokens)
    query_index = first_row + jnp.arange(tokens, dtype=jnp.int32)
    starts = jnp.sum((segment_ids[None, :] < own_segs[:, None]).astype(jnp.int32), axis=1)
    positions = query_index - starts
    normed = normalize(hidden, norm_attn).astype(jnp.bfloat16)
    query_heads = w_query.shape[1] // HEAD_DIM
    kv_heads = w_key.shape[1] // HEAD_DIM
    queries = jnp.dot(normed, w_query, preferred_element_type=jnp.float32)
    key_raw = jnp.dot(normed, w_key, preferred_element_type=jnp.float32)
    value_proj = jnp.dot(normed, w_value, preferred_element_type=jnp.float32).astype(jnp.bfloat16)
    kv_cache = jnp.stack([key_raw.astype(jnp.bfloat16), value_proj], axis=1)
    queries = rotary(queries.reshape(tokens, query_heads, HEAD_DIM), positions)
    key_rot = rotary(key_raw.reshape(tokens, kv_heads, HEAD_DIM), positions)
    queries = queries.astype(jnp.bfloat16)
    key_rot = key_rot.astype(jnp.bfloat16).reshape(tokens, kv_heads * HEAD_DIM)
    return queries, key_rot, value_proj, kv_cache, own_segs, query_index, starts


def attend_all(queries, keys_all, values_all, query_index, starts):
    tokens, query_heads, _ = queries.shape
    total = keys_all.shape[0]
    kv_heads = keys_all.shape[1] // HEAD_DIM
    grouped = queries.reshape(tokens, kv_heads, query_heads // kv_heads, HEAD_DIM)
    keys = keys_all.reshape(total, kv_heads, HEAD_DIM)
    values = values_all.reshape(total, kv_heads, HEAD_DIM)
    scores = (
        jnp.einsum("tkgd,skd->kgts", grouped, keys, preferred_element_type=jnp.float32)
        * SCORE_SCALE
    )
    key_index = jnp.arange(total, dtype=jnp.int32)
    allowed = (key_index[None, :] <= query_index[:, None]) & (
        key_index[None, :] >= starts[:, None]
    )
    masked = jnp.where(allowed, scores, -1e30)
    top = jnp.max(masked, axis=-1, keepdims=True)
    weights = jnp.where(allowed, jnp.exp(masked - top), 0.0)
    weight_sum = jnp.sum(weights, axis=-1)
    mixed = jnp.einsum(
        "kgts,skd->kgtd",
        weights.astype(jnp.bfloat16),
        values,
        preferred_element_type=jnp.float32,
    )
    attended = (mixed / weight_sum[..., None]).transpose(2, 0, 1, 3)
    return attended.reshape(tokens, query_heads * HEAD_DIM).astype(jnp.bfloat16)


def expert_gates(routes, gates, experts):
    hit = routes[:, :, None] == jnp.arange(experts, dtype=jnp.int32)[None, None, :]
    return jnp.sum(jnp.where(hit, gates[:, :, None], 0.0), axis=1)


def flip(seq_index, mask):
    bits = [seq_index // 4, (seq_index // 2) % 2, seq_index % 2]
    bits = [1 - bit if (mask >> (2 - n)) & 1 else bit for n, bit in enumerate(bits)]
    return bits[0] * 4 + bits[1] * 2 + bits[2]


CORE, XDIR, YDIR = 1, 2, 4


def experts_kernel(
    normed_ref, residual_ref, gates_ref, wg_hbm, wu_hbm, wd_hbm, out_ref,
    rows, weights, downs, act, parts, from_core, first, second, from_tp,
    weight_sem, send_sem, row_sem, core_sem, first_sem, second_sem, tp_sem, out_sem,
):
    me, tp = lax.axis_index("seq"), lax.axis_index("tp")
    n_tp = rows.shape[1]
    block = rows.shape[2]
    slots = weights.shape[0]
    units = weights.shape[2] // 2
    width = rows.shape[3]
    seq_peer = {mask: (flip(me, mask), tp) for mask in (CORE, XDIR, YDIR)}
    tp_peer = {k: (me, (tp + k) % n_tp) for k in range(1, n_tp)}

    loads = []
    for n in range(slots):
        for half, source in ((0, wg_hbm), (1, wu_hbm)):
            loads.append(
                pltpu.make_async_copy(
                    source.at[n],
                    weights.at[n, :, pl.ds(half * units, units)],
                    weight_sem.at[2 * n + half],
                )
            )
    loads.append(pltpu.make_async_copy(wd_hbm, downs, weight_sem.at[2 * slots]))
    for load in loads:
        load.start()

    barrier = pltpu.get_barrier_semaphore()
    peers = list(seq_peer.values()) + list(tp_peer.values())
    for peer in peers:
        pl.semaphore_signal(
            barrier, inc=1, device_id=peer, device_id_type=pl.DeviceIdType.MESH
        )
    pl.semaphore_wait(barrier, len(peers))

    sent = []

    def send(source, target, sem, peer):
        copy = pltpu.make_async_remote_copy(
            src_ref=source,
            dst_ref=target,
            send_sem=send_sem.at[len(sent)],
            recv_sem=sem,
            device_id=peer,
            device_id_type=pl.DeviceIdType.MESH,
        )
        copy.start()
        sent.append(copy)

    def arrived(target, sem):
        pltpu.make_async_remote_copy(
            src_ref=target,
            dst_ref=target,
            send_sem=send_sem.at[0],
            recv_sem=sem,
            device_id=seq_peer[CORE],
            device_id_type=pl.DeviceIdType.MESH,
        ).wait_recv()

    def pass_on(mask, k, way, source=None):
        source = rows.at[mask, k] if source is None else source
        send(source, rows.at[mask ^ way, k], row_sem.at[mask ^ way, k], seq_peer[way])

    def take(mask, k):
        arrived(rows.at[mask, k], row_sem.at[mask, k])

    rows[0, 0] = normed_ref[...]
    for k in (2, 1, 3):
        back = n_tp - k
        send(normed_ref, rows.at[0, back], row_sem.at[0, back], tp_peer[k])
    for way in (XDIR, YDIR, CORE):
        pass_on(0, 0, way, normed_ref)

    def handle_sides(k):
        take(XDIR, k)
        if k >= 2:
            pass_on(XDIR, k, YDIR)
        take(YDIR, k)
        if k < 2:
            pass_on(YDIR, k, XDIR)
        pass_on(XDIR, k, CORE)
        pass_on(YDIR, k, CORE)

    def compute(mask):
        group = rows[mask].reshape(n_tp * block, width)
        seq_row = flip(me, mask) * (n_tp * block)
        gate = jnp.concatenate(
            [
                gates_ref[pl.ds(pl.multiple_of(seq_row + ((tp + k) % n_tp) * block, block), block), :]
                for k in range(n_tp)
            ],
            axis=0,
        )
        for n in range(slots):
            both = jnp.dot(group, weights[n], preferred_element_type=jnp.float32)
            gate_val, up_val = both[:, :units], both[:, units:]
            scale = gate[:, n : n + 1]
            value = gate_val / (1.0 + jnp.exp(-gate_val)) * up_val * scale
            act[:, n * units : (n + 1) * units] = jnp.where(scale > 0, value, 0.0).astype(
                jnp.bfloat16
            )
        step = 256
        for column in range(0, width, step):
            piece = jnp.dot(
                act[...],
                downs[:, column : column + step],
                preferred_element_type=jnp.float32,
            ).astype(jnp.bfloat16)
            for k in range(n_tp):
                parts[mask, k, :, column : column + step] = piece[k * block : (k + 1) * block]

    def give_core(mask):
        send(parts.at[mask], from_core.at[mask // 2], core_sem.at[mask // 2], seq_peer[CORE])

    def add(mask, k, extra):
        parts[mask, k] = (
            parts[mask, k].astype(jnp.float32) + extra.astype(jnp.float32)
        ).astype(jnp.bfloat16)

    def add_core(mask):
        arrived(from_core.at[mask // 2], core_sem.at[mask // 2])
        for k in range(n_tp):
            add(mask, k, from_core[mask // 2, k])

    for k in (1, 3, 2):
        take(0, k)
        for way in (XDIR, YDIR, CORE):
            pass_on(0, k, way)
    handle_sides(0)
    handle_sides(1)
    for load in loads:
        load.wait()
    compute(0)
    handle_sides(3)
    handle_sides(2)
    for k in range(n_tp):
        take(CORE, k)
    compute(1)
    give_core(1)
    compute(2)
    for k in range(n_tp):
        take(XDIR + CORE, k)
    compute(3)
    give_core(3)
    for k in range(n_tp):
        take(YDIR + XDIR, k)
        pass_on(YDIR + XDIR, k, CORE)
    for k in range(n_tp):
        take(YDIR + CORE, k)
    compute(5)
    give_core(5)
    compute(4)
    for k in range(n_tp):
        take(YDIR + XDIR + CORE, k)
    compute(7)
    give_core(7)
    compute(6)

    early = ((XDIR, YDIR, (1, 0)), (YDIR, XDIR, (2, 3)))

    def give_first(mask, way, ks):
        for k in ks:
            slot = 0 if mask == way else 1
            send(parts.at[mask, k], first.at[slot, k], first_sem.at[slot, k], seq_peer[way])

    for way, other, ks in early:
        add_core(way)
        give_first(way, way, ks)
    add_core(XDIR + YDIR)
    for way, other, ks in early:
        give_first(XDIR + YDIR, way, ks)
    add_core(0)
    for way, other, ks in early:
        for k in ks:
            arrived(first.at[1, k], first_sem.at[1, k])
            add(other, k, first[1, k])
            send(parts.at[other, k], second.at[k], second_sem.at[k], seq_peer[other])
    for k in (2, 1, 3, 0):
        arrived(first.at[0, k], first_sem.at[0, k])
        add(0, k, first[0, k])
    for k in (2, 1, 3, 0):
        arrived(second.at[k], second_sem.at[k])
        add(0, k, second[k])
        if k:
            back = n_tp - k
            send(parts.at[0, k], from_tp.at[back], tp_sem.at[back], tp_peer[k])
    total = residual_ref[...].astype(jnp.float32) + parts[0, 0].astype(jnp.float32)
    for k in (1, 3, 2):
        arrived(from_tp.at[k], tp_sem.at[k])
        total = total + from_tp[k].astype(jnp.float32)
    own = out_ref.at[pl.ds(pl.multiple_of(tp * block, block), block)]
    own[...] = total.astype(jnp.bfloat16)
    for k in (2, 1, 3):
        send(own, own, out_sem.at[n_tp - k], tp_peer[k])
    for k in (1, 3, 2):
        start = pl.multiple_of(((tp + k) % n_tp) * block, block)
        arrived(out_ref.at[pl.ds(start, block)], out_sem.at[k])
    for copy in sent:
        copy.wait_send()


def run_experts(normed, residual, own_gates, w_gate, w_up, w_down):
    block, width = normed.shape
    n_tp = lax.axis_size("tp")
    n_seq = lax.axis_size("seq")
    slots, _, units = w_gate.shape
    bf16 = jnp.bfloat16
    flops = 2 * own_gates.shape[0] * slots * width * units * 3
    return pl.pallas_call(
        experts_kernel,
        out_shape=jax.ShapeDtypeStruct((n_tp * block, width), bf16),
        in_specs=[pl.BlockSpec(memory_space=pltpu.VMEM)] * 3
        + [pl.BlockSpec(memory_space=pl.ANY)] * 3,
        out_specs=pl.BlockSpec(memory_space=pltpu.VMEM),
        scratch_shapes=[
            pltpu.VMEM((n_seq, n_tp, block, width), bf16),
            pltpu.VMEM((slots, width, 2 * units), bf16),
            pltpu.VMEM((slots * units, width), bf16),
            pltpu.VMEM((n_tp * block, slots * units), bf16),
            pltpu.VMEM((n_seq, n_tp, block, width), bf16),
            pltpu.VMEM((n_seq // 2, n_tp, block, width), bf16),
            pltpu.VMEM((2, n_tp, block, width), bf16),
            pltpu.VMEM((n_tp, block, width), bf16),
            pltpu.VMEM((n_tp, block, width), bf16),
            pltpu.SemaphoreType.DMA((2 * slots + 1,)),
            pltpu.SemaphoreType.DMA((64,)),
            pltpu.SemaphoreType.DMA((n_seq, n_tp)),
            pltpu.SemaphoreType.DMA((n_seq // 2,)),
            pltpu.SemaphoreType.DMA((2, n_tp)),
            pltpu.SemaphoreType.DMA((n_tp,)),
            pltpu.SemaphoreType.DMA((n_tp,)),
            pltpu.SemaphoreType.DMA((n_tp,)),
        ],
        compiler_params=pltpu.CompilerParams(
            collective_id=0, has_side_effects=True, vmem_limit_bytes=40 * 1024 * 1024
        ),
        cost_estimate=pl.CostEstimate(
            flops=flops, bytes_accessed=4 * 1024 * 1024, transcendentals=0
        ),
        name="experts",
    )(normed, residual, own_gates, w_gate, w_up, w_down.reshape(slots * units, width))


def per_device(
    hidden,
    segment_ids,
    routes,
    gates,
    norm_attn,
    norm_moe,
    w_query,
    w_key,
    w_value,
    w_out,
    w_gate,
    w_up,
    w_down,
):
    tokens, width = hidden.shape
    slots = w_gate.shape[0]
    part = tokens // lax.axis_size("tp")
    queries, key_rot, value_proj, kv_cache, own_segs, query_index, starts = attention_inputs(
        hidden, segment_ids, norm_attn, w_query, w_key, w_value
    )
    table = expert_gates(routes, gates, EXPERTS)
    high = table.astype(jnp.bfloat16)
    low = (table - high.astype(jnp.float32)).astype(jnp.bfloat16)
    kv_width = key_rot.shape[1]
    gathered = lax.all_gather(
        jnp.concatenate([key_rot, value_proj, high, low], axis=1), "seq", axis=0, tiled=True
    )
    keys_all, values_all = gathered[:, :kv_width], gathered[:, kv_width : 2 * kv_width]
    first_column = 2 * kv_width + lax.axis_index("seq") * slots
    own_gates = lax.dynamic_slice_in_dim(gathered, first_column, slots, axis=1).astype(
        jnp.float32
    ) + lax.dynamic_slice_in_dim(gathered, first_column + EXPERTS, slots, axis=1).astype(
        jnp.float32
    )
    attended = attend_all(queries, keys_all, values_all, query_index, starts)
    partial_out = jnp.dot(attended, w_out, preferred_element_type=jnp.float32)
    mixed = lax.psum_scatter(
        partial_out.astype(jnp.bfloat16), "tp", scatter_dimension=0, tiled=True
    )
    own_part = lax.dynamic_slice_in_dim(hidden, lax.axis_index("tp") * part, part)
    residual = (own_part.astype(jnp.float32) + mixed.astype(jnp.float32)).astype(jnp.bfloat16)
    normed = normalize(residual, norm_moe).astype(jnp.bfloat16)
    hidden_out = run_experts(normed, residual, own_gates, w_gate, w_up, w_down)
    return hidden_out, kv_cache


def solution(mesh):
    whole_rows = mesh.shape["seq"] == 8 and mesh.shape["tp"] == 4
    return jax.shard_map(
        per_device if whole_rows else per_device_routed,
        mesh=mesh,
        in_specs=(
            P("seq", None),
            P(),
            P("seq", None),
            P("seq", None),
            P(),
            P(),
            P(None, "tp"),
            P(None, "tp"),
            P(None, "tp"),
            P("tp", None),
            P("seq", None, "tp"),
            P("seq", None, "tp"),
            P("seq", "tp", None),
        ),
        out_specs=(P("seq", None), P("seq", None, "tp")),
        check_vma=False,
    )
```

```python
import jax
import jax.numpy as jnp
from jax import lax
from jax.experimental import pallas as pl
from jax.experimental.pallas import tpu as pltpu
from jax.sharding import PartitionSpec as P

HEAD_DIM = 64
EXPERTS = 32


EPS = 1e-06
SCORE_SCALE = 0.015625


def normalize(values, gain):
    widened = values.astype(jnp.float32)
    return (
        widened
        * lax.rsqrt(jnp.mean(widened * widened, axis=-1, keepdims=True) + EPS)
        * gain.astype(jnp.float32)
    )


def rotary(tensor, positions):
    half_dim = tensor.shape[-1] // 2
    frequencies = 10000.0 ** (-jnp.arange(half_dim, dtype=jnp.float32) * 2.0 / tensor.shape[-1])
    angles = positions.astype(jnp.float32)[:, None] * frequencies[None, :]
    cosine = jnp.cos(angles)[:, None, :]
    sine_part = jnp.sin(angles)[:, None, :]
    lower_half = tensor[..., :half_dim]
    upper_half = tensor[..., half_dim:]
    return jnp.concatenate(
        [
            lower_half * cosine - upper_half * sine_part,
            upper_half * cosine + lower_half * sine_part,
        ],
        axis=-1,
    )


def segment_positions(segment_ids):
    index_all = jnp.arange(segment_ids.shape[0], dtype=jnp.int32)
    changed = jnp.concatenate([jnp.ones((1,), jnp.bool_), segment_ids[1:] != segment_ids[:-1]])
    starts = lax.cummax(jnp.where(changed, index_all, 0), axis=0)
    return index_all - starts


def per_device_routed(
    hidden,
    segment_ids,
    routes,
    gates,
    norm_attn,
    norm_moe,
    w_query,
    w_key,
    w_value,
    w_out,
    w_gate,
    w_up,
    w_down,
):
    tokens = hidden.shape[0]
    model_width = hidden.shape[1]
    first_row = lax.axis_index("seq") * tokens
    positions = lax.dynamic_slice_in_dim(segment_positions(segment_ids), first_row, tokens)
    own_segs = lax.dynamic_slice_in_dim(segment_ids, first_row, tokens)
    normed = normalize(hidden, norm_attn).astype(jnp.bfloat16)
    query_heads = w_query.shape[1] // HEAD_DIM
    kv_heads = w_key.shape[1] // HEAD_DIM
    group_size = query_heads // kv_heads
    queries = jnp.dot(normed, w_query, preferred_element_type=jnp.float32).reshape(
        tokens, query_heads, HEAD_DIM
    )
    queries = (
        rotary(queries, positions)
        .astype(jnp.bfloat16)
        .reshape(tokens, kv_heads, group_size, HEAD_DIM)
    )
    key_raw = jnp.dot(normed, w_key, preferred_element_type=jnp.float32).reshape(
        tokens, kv_heads, HEAD_DIM
    )
    value_proj = jnp.dot(normed, w_value, preferred_element_type=jnp.float32).astype(jnp.bfloat16)
    kv_cache = jnp.stack(
        [key_raw.reshape(tokens, kv_heads * HEAD_DIM).astype(jnp.bfloat16), value_proj], axis=1
    )
    key_rot = rotary(key_raw, positions).astype(jnp.bfloat16)
    value_heads = value_proj.reshape(tokens, kv_heads, HEAD_DIM)
    query_index = first_row + jnp.arange(tokens, dtype=jnp.int32)
    last_query = first_row + tokens - 1
    lowest_seg = own_segs[0]

    def attend(carried, key_rows, value_rows, key_start, key_segs):
        running_max, weight_sum, accumulated = carried
        scores = (
            jnp.einsum("tkgd,skd->kgts", queries, key_rows, preferred_element_type=jnp.float32)
            * SCORE_SCALE
        )
        key_index = key_start + jnp.arange(key_rows.shape[0], dtype=jnp.int32)
        allowed = (own_segs[:, None] == key_segs[None, :]) & (
            query_index[:, None] >= key_index[None, :]
        )
        masked = jnp.where(allowed, scores, -1e30)
        new_max = jnp.maximum(running_max, jnp.max(masked, axis=-1))
        weights = jnp.where(allowed, jnp.exp(masked - new_max[..., None]), 0.0)
        factor = jnp.exp(running_max - new_max)
        weight_sum = weight_sum * factor + jnp.sum(weights, axis=-1)
        accumulated = accumulated * factor[..., None] + jnp.einsum(
            "kgts,skd->kgtd",
            weights.astype(jnp.bfloat16),
            value_rows,
            preferred_element_type=jnp.float32,
        )
        return (new_max, weight_sum, accumulated)

    start_state = (
        jnp.full((kv_heads, group_size, tokens), -1e30, jnp.float32),
        jnp.zeros((kv_heads, group_size, tokens), jnp.float32),
        jnp.zeros((kv_heads, group_size, tokens, HEAD_DIM), jnp.float32),
    )
    keys_all = lax.all_gather(key_rot, "seq", axis=0, tiled=True)
    values_all = lax.all_gather(value_heads, "seq", axis=0, tiled=True)
    block_total = keys_all.shape[0] // tokens

    def visit_block(block_index, state_now):
        key_start = block_index * tokens
        key_rows = lax.dynamic_slice_in_dim(keys_all, block_index * tokens, tokens)
        value_rows = lax.dynamic_slice_in_dim(values_all, block_index * tokens, tokens)
        key_segs = lax.dynamic_slice_in_dim(segment_ids, key_start, tokens)
        relevant = (key_start <= last_query) & (key_segs[tokens - 1] >= lowest_seg)
        return lax.cond(
            relevant,
            lambda inner: attend(inner, key_rows, value_rows, key_start, key_segs),
            lambda inner: inner,
            state_now,
        )

    running_max, weight_sum, accumulated = lax.fori_loop(0, block_total, visit_block, start_state)
    attended = (
        (accumulated / weight_sum[..., None])
        .transpose(2, 0, 1, 3)
        .reshape(tokens, query_heads * HEAD_DIM)
    )
    attended = attended.astype(jnp.bfloat16)
    partial_out = jnp.dot(attended, w_out, preferred_element_type=jnp.float32)
    attn_mixed = lax.psum(partial_out.astype(jnp.bfloat16), "tp").astype(jnp.float32)
    residual = (hidden.astype(jnp.float32) + attn_mixed).astype(jnp.bfloat16)
    normed_moe = normalize(residual, norm_moe).astype(jnp.bfloat16)
    route_count = routes.shape[1]
    slots_dev = w_gate.shape[0]
    seq_count = lax.axis_size("seq")
    slot_total = slots_dev * seq_count
    copies = slot_total // EXPERTS
    block_rows = tokens // copies
    capacity = 2 * block_rows * route_count // EXPERTS
    copy_of = (jnp.arange(tokens, dtype=jnp.int32) // block_rows)[:, None]
    slot_of = routes + EXPERTS * copy_of
    flat_expert = routes.reshape(copies, block_rows * route_count)
    onehot = (
        flat_expert[:, :, None] == jnp.arange(EXPERTS, dtype=jnp.int32)[None, None, :]
    ).astype(jnp.int32)
    before = jnp.cumsum(onehot, axis=1) - onehot
    slot_rank = jnp.sum(before * onehot, axis=2).reshape(tokens, route_count)
    target = slot_of * capacity + slot_rank
    token_ids = jnp.broadcast_to(
        jnp.arange(tokens, dtype=jnp.int32)[:, None], (tokens, route_count)
    )
    source = (
        jnp.full((slot_total * capacity,), tokens, jnp.int32)
        .at[target.reshape(-1)]
        .set(token_ids.reshape(-1))
    )
    padded_rows = jnp.concatenate([normed_moe, jnp.zeros((1, normed_moe.shape[1]), jnp.bfloat16)])
    outbound = padded_rows[source].reshape(seq_count, slots_dev, capacity, normed_moe.shape[1])
    arrived = lax.all_to_all(outbound, "seq", split_axis=0, concat_axis=0, tiled=True)
    gate_val = jnp.einsum("jsrd,sdf->jsrf", arrived, w_gate, preferred_element_type=jnp.float32)
    up_val = jnp.einsum("jsrd,sdf->jsrf", arrived, w_up, preferred_element_type=jnp.float32)
    activated = (jax.nn.silu(gate_val) * up_val).astype(jnp.bfloat16)
    group_part = jnp.einsum("jsrf,sfd->jsrd", activated, w_down, preferred_element_type=jnp.float32)
    result = group_part.astype(jnp.bfloat16)
    returned = lax.all_to_all(result, "seq", split_axis=0, concat_axis=0, tiled=True).reshape(
        slot_total * capacity, model_width
    )
    picked = returned[target]
    combined = jnp.einsum(
        "tk,tkd->td",
        gates,
        picked,
        preferred_element_type=jnp.float32,
        precision=lax.Precision.HIGHEST,
    )
    expert_sum = lax.psum(combined.astype(jnp.bfloat16), "tp").astype(jnp.float32)
    hidden_out = (residual.astype(jnp.float32) + expert_sum).astype(jnp.bfloat16)
    return (hidden_out, kv_cache)


def attention_inputs(hidden, segment_ids, norm_attn, w_query, w_key, w_value):
    tokens = hidden.shape[0]
    first_row = lax.axis_index("seq") * tokens
    own_segs = lax.dynamic_slice_in_dim(segment_ids, first_row, tokens)
    query_index = first_row + jnp.arange(tokens, dtype=jnp.int32)
    starts = jnp.sum((segment_ids[None, :] < own_segs[:, None]).astype(jnp.int32), axis=1)
    positions = query_index - starts
    normed = normalize(hidden, norm_attn).astype(jnp.bfloat16)
    query_heads = w_query.shape[1] // HEAD_DIM
    kv_heads = w_key.shape[1] // HEAD_DIM
    queries = jnp.dot(normed, w_query, preferred_element_type=jnp.float32)
    key_raw = jnp.dot(normed, w_key, preferred_element_type=jnp.float32)
    value_proj = jnp.dot(normed, w_value, preferred_element_type=jnp.float32).astype(jnp.bfloat16)
    kv_cache = jnp.stack([key_raw.astype(jnp.bfloat16), value_proj], axis=1)
    queries = rotary(queries.reshape(tokens, query_heads, HEAD_DIM), positions)
    key_rot = rotary(key_raw.reshape(tokens, kv_heads, HEAD_DIM), positions)
    queries = queries.astype(jnp.bfloat16)
    key_rot = key_rot.astype(jnp.bfloat16).reshape(tokens, kv_heads * HEAD_DIM)
    return queries, key_rot, value_proj, kv_cache, own_segs, query_index, starts


def expert_gates(routes, gates, experts):
    hit = routes[:, :, None] == jnp.arange(experts, dtype=jnp.int32)[None, None, :]
    return jnp.sum(jnp.where(hit, gates[:, :, None], 0.0), axis=1)


def normalize_rows(values, gain):
    widened = values.astype(jnp.float32)
    mean = jnp.mean(widened * widened, axis=-1, keepdims=True)
    return widened * lax.rsqrt(mean + EPS) * gain.astype(jnp.float32)


def flip(seq_index, mask):
    bits = [seq_index // 4, (seq_index // 2) % 2, seq_index % 2]
    bits = [1 - bit if (mask >> (2 - n)) & 1 else bit for n, bit in enumerate(bits)]
    return bits[0] * 4 + bits[1] * 2 + bits[2]


CORE, XDIR, YDIR = 1, 2, 4


def layer_kernel(
    query_ref, kv_ref, table_ref, starts_ref, hidden_ref, norm_ref, wo_ref,
    wg_hbm, wu_hbm, wd_hbm, out_ref,
    kv, table, top, norm_sum, mixed, partial_out, from_heads, residual, normed_ref,
    kv_sem, table_sem, heads_sem,
    rows, weights, downs, act, parts, from_core, first, second, from_tp,
    weight_sem, send_sem, row_sem, core_sem, first_sem, second_sem, tp_sem, out_sem,
):
    me, tp = lax.axis_index("seq"), lax.axis_index("tp")
    n_tp = rows.shape[1]
    block = rows.shape[2]
    slots = weights.shape[0]
    units = weights.shape[2] // 2
    width = rows.shape[3]
    seq_peer = {mask: (flip(me, mask), tp) for mask in (CORE, XDIR, YDIR)}
    tp_peer = {k: (me, (tp + k) % n_tp) for k in range(1, n_tp)}

    loads = []
    for n in range(slots):
        for half, source in ((0, wg_hbm), (1, wu_hbm)):
            loads.append(
                pltpu.make_async_copy(
                    source.at[n],
                    weights.at[n, :, pl.ds(half * units, units)],
                    weight_sem.at[2 * n + half],
                )
            )
    loads.append(pltpu.make_async_copy(wd_hbm, downs, weight_sem.at[2 * slots]))
    for load in loads:
        load.start()

    barrier = pltpu.get_barrier_semaphore()
    peers = list(seq_peer.values()) + list(tp_peer.values())
    for peer in peers:
        pl.semaphore_signal(
            barrier, inc=1, device_id=peer, device_id_type=pl.DeviceIdType.MESH
        )
    pl.semaphore_wait(barrier, len(peers))

    sent = []

    def send(source, target, sem, peer):
        copy = pltpu.make_async_remote_copy(
            src_ref=source,
            dst_ref=target,
            send_sem=send_sem.at[len(sent)],
            recv_sem=sem,
            device_id=peer,
            device_id_type=pl.DeviceIdType.MESH,
        )
        copy.start()
        sent.append(copy)

    def arrived(target, sem):
        pltpu.make_async_remote_copy(
            src_ref=target,
            dst_ref=target,
            send_sem=send_sem.at[0],
            recv_sem=sem,
            device_id=seq_peer[CORE],
            device_id_type=pl.DeviceIdType.MESH,
        ).wait_recv()

    def spread(buffer, sems, parts_of):
        def go(mask, k, way):
            send(buffer.at[mask, k], buffer.at[mask ^ way, k], sems.at[mask ^ way, k], seq_peer[way])

        def take(mask, k):
            arrived(buffer.at[mask, k], sems.at[mask, k])

        def sides(k):
            take(XDIR, k)
            if k >= parts_of // 2:
                go(XDIR, k, YDIR)
            take(YDIR, k)
            if k < parts_of // 2:
                go(YDIR, k, XDIR)
            go(XDIR, k, CORE)
            go(YDIR, k, CORE)

        return go, take, sides

    halves = (0, 1)
    kv_go, kv_take, kv_sides = spread(kv, kv_sem, 2)
    table_go, table_take, table_sides = spread(table, table_sem, 2)
    half = kv.shape[2]
    for k in halves:
        kv[0, k] = kv_ref[k * half : (k + 1) * half, :]
        table[0, k] = table_ref[k * half : (k + 1) * half, :]
    for k in halves:
        for way in (XDIR, YDIR, CORE):
            kv_go(0, k, way)
    for k in halves:
        for way in (XDIR, YDIR, CORE):
            table_go(0, k, way)

    tokens = 2 * half
    kv_width = kv.shape[3] // 2
    heads = query_ref.shape[0] // tokens
    top[...] = jnp.full(top.shape, -1e30, jnp.float32)
    norm_sum[...] = jnp.zeros(norm_sum.shape, jnp.float32)
    mixed[...] = jnp.zeros(mixed.shape, jnp.float32)

    def attend(mask):
        block_kv = kv[mask].reshape(tokens, 2 * kv_width)
        keys, values = block_kv[:, :kv_width], block_kv[:, kv_width:]
        query_index = me * tokens + lax.broadcasted_iota(jnp.int32, (tokens, tokens), 0)
        key_index = flip(me, mask) * tokens + lax.broadcasted_iota(
            jnp.int32, (tokens, tokens), 1
        )
        allowed = (key_index <= query_index) & (key_index >= starts_ref[...])

        for head in range(heads):
            span = pl.ds(head * tokens, tokens)
            scores = (
                lax.dot_general(
                    query_ref[span, :],
                    keys,
                    (((1,), (1,)), ((), ())),
                    preferred_element_type=jnp.float32,
                )
                * SCORE_SCALE
            )
            masked = jnp.where(allowed, scores, -1e30)
            old_top = top[span, :]
            new_top = jnp.maximum(old_top, jnp.max(masked, axis=1, keepdims=True))
            weights_now = jnp.where(allowed, jnp.exp(masked - new_top), 0.0)
            factor = jnp.exp(old_top - new_top)
            top[span, :] = new_top
            norm_sum[span, :] = norm_sum[span, :] * factor + jnp.sum(
                weights_now, axis=1, keepdims=True
            )
            mixed[span, :] = mixed[span, :] * factor + jnp.dot(
                weights_now.astype(jnp.bfloat16), values, preferred_element_type=jnp.float32
            )

    attend(0)
    for k in halves:
        kv_sides(k)
    for k in halves:
        kv_take(CORE, k)
    attend(XDIR)
    attend(YDIR)
    for k in halves:
        kv_take(XDIR + YDIR, k)
        kv_go(XDIR + YDIR, k, CORE)
    attend(CORE)
    for k in halves:
        table_sides(k)
    attend(XDIR + YDIR)
    for mask in (XDIR + CORE, YDIR + CORE, XDIR + YDIR + CORE):
        for k in halves:
            kv_take(mask, k)
        attend(mask)
    for k in halves:
        table_take(XDIR + YDIR, k)
        table_go(XDIR + YDIR, k, CORE)

    attended = jnp.concatenate(
        [
            (mixed[pl.ds(h * tokens, tokens), :] / norm_sum[pl.ds(h * tokens, tokens), :]).astype(
                jnp.bfloat16
            )
            for h in range(heads)
        ],
        axis=1,
    )
    step = 256
    for column in range(0, width, step):
        partial_out[:, column : column + step] = jnp.dot(
            attended, wo_ref[:, column : column + step], preferred_element_type=jnp.float32
        ).astype(jnp.bfloat16)

    def block_rows(k):
        return pl.ds(pl.multiple_of(((tp + k) % n_tp) * block, block), block)

    for k in (2, 1, 3):
        back = n_tp - k
        send(partial_out.at[block_rows(k)], from_heads.at[back], heads_sem.at[back], tp_peer[k])
    summed = partial_out[block_rows(0), :].astype(jnp.float32)
    for k in (1, 3, 2):
        arrived(from_heads.at[k], heads_sem.at[k])
        summed = summed + from_heads[k].astype(jnp.float32)
    added = hidden_ref[block_rows(0), :].astype(jnp.float32) + summed
    residual[...] = added.astype(jnp.bfloat16)
    normed_ref[...] = normalize_rows(residual[...], norm_ref[...]).astype(jnp.bfloat16)

    pass_on, take, handle_sides = spread(rows, row_sem, n_tp)
    rows[0, 0] = normed_ref[...]
    for k in (2, 1, 3):
        back = n_tp - k
        send(rows.at[0, 0], rows.at[0, back], row_sem.at[0, back], tp_peer[k])
    for way in (XDIR, YDIR, CORE):
        pass_on(0, 0, way)
    for mask in (CORE, XDIR + CORE, YDIR + CORE, XDIR + YDIR + CORE):
        for k in halves:
            table_take(mask, k)

    def compute(mask):
        group = rows[mask].reshape(n_tp * block, width)
        gate = jnp.concatenate(
            [
                table[
                    mask,
                    ((tp + k) % n_tp) // 2,
                    pl.ds(pl.multiple_of(((tp + k) % 2) * block, block), block),
                    :,
                ]
                for k in range(n_tp)
            ],
            axis=0,
        ).astype(jnp.float32)
        lane = lax.broadcasted_iota(jnp.int32, gate.shape, 1)
        for n in range(slots):
            both = jnp.dot(group, weights[n], preferred_element_type=jnp.float32)
            gate_val, up_val = both[:, :units], both[:, units:]
            column = me * slots + n
            chosen = (lane == column) | (lane == column + EXPERTS)
            scale = jnp.sum(jnp.where(chosen, gate, 0.0), axis=1, keepdims=True)
            value = gate_val / (1.0 + jnp.exp(-gate_val)) * up_val * scale
            act[:, n * units : (n + 1) * units] = jnp.where(scale > 0, value, 0.0).astype(
                jnp.bfloat16
            )
        for column in range(0, width, step):
            piece = jnp.dot(
                act[...],
                downs[:, column : column + step],
                preferred_element_type=jnp.float32,
            ).astype(jnp.bfloat16)
            for k in range(n_tp):
                parts[mask, k, :, column : column + step] = piece[k * block : (k + 1) * block]

    def give_core(mask):
        send(parts.at[mask], from_core.at[mask // 2], core_sem.at[mask // 2], seq_peer[CORE])

    def add(mask, k, extra):
        parts[mask, k] = (
            parts[mask, k].astype(jnp.float32) + extra.astype(jnp.float32)
        ).astype(jnp.bfloat16)

    def add_core(mask):
        arrived(from_core.at[mask // 2], core_sem.at[mask // 2])
        for k in range(n_tp):
            add(mask, k, from_core[mask // 2, k])

    for k in (1, 3, 2):
        take(0, k)
        for way in (XDIR, YDIR, CORE):
            pass_on(0, k, way)
    handle_sides(0)
    handle_sides(1)
    for load in loads:
        load.wait()
    compute(0)
    handle_sides(3)
    handle_sides(2)
    for k in range(n_tp):
        take(CORE, k)
    compute(1)
    give_core(1)
    compute(2)
    for k in range(n_tp):
        take(XDIR + CORE, k)
    compute(3)
    give_core(3)
    for k in range(n_tp):
        take(YDIR + XDIR, k)
        pass_on(YDIR + XDIR, k, CORE)
    for k in range(n_tp):
        take(YDIR + CORE, k)
    compute(5)
    give_core(5)
    compute(4)
    for k in range(n_tp):
        take(YDIR + XDIR + CORE, k)
    compute(7)
    give_core(7)
    compute(6)

    early = ((XDIR, YDIR, (1, 0)), (YDIR, XDIR, (2, 3)))

    def give_first(mask, way, ks):
        for k in ks:
            slot = 0 if mask == way else 1
            send(parts.at[mask, k], first.at[slot, k], first_sem.at[slot, k], seq_peer[way])

    for way, other, ks in early:
        add_core(way)
        give_first(way, way, ks)
    add_core(XDIR + YDIR)
    for way, other, ks in early:
        give_first(XDIR + YDIR, way, ks)
    add_core(0)
    for way, other, ks in early:
        for k in ks:
            arrived(first.at[1, k], first_sem.at[1, k])
            add(other, k, first[1, k])
            send(parts.at[other, k], second.at[k], second_sem.at[k], seq_peer[other])
    for k in (2, 1, 3, 0):
        arrived(first.at[0, k], first_sem.at[0, k])
        add(0, k, first[0, k])
    for k in (2, 1, 3, 0):
        arrived(second.at[k], second_sem.at[k])
        add(0, k, second[k])
        if k:
            back = n_tp - k
            send(parts.at[0, k], from_tp.at[back], tp_sem.at[back], tp_peer[k])
    total = residual[...].astype(jnp.float32) + parts[0, 0].astype(jnp.float32)
    for k in (1, 3, 2):
        arrived(from_tp.at[k], tp_sem.at[k])
        total = total + from_tp[k].astype(jnp.float32)
    own = out_ref.at[pl.ds(pl.multiple_of(tp * block, block), block)]
    own[...] = total.astype(jnp.bfloat16)
    for k in (2, 1, 3):
        send(own, own, out_sem.at[n_tp - k], tp_peer[k])
    for k in (1, 3, 2):
        start = pl.multiple_of(((tp + k) % n_tp) * block, block)
        arrived(out_ref.at[pl.ds(start, block)], out_sem.at[k])
    for copy in sent:
        copy.wait_send()


def run_layer(queries, kv, table, starts, hidden, norm_moe, w_out, w_gate, w_up, w_down):
    tokens, width = hidden.shape
    n_tp = lax.axis_size("tp")
    n_seq = lax.axis_size("seq")
    block = tokens // n_tp
    slots, _, units = w_gate.shape
    lanes = queries.shape[1]
    bf16, f32 = jnp.bfloat16, jnp.float32
    flops = 2 * n_seq * tokens * slots * width * units * 3
    return pl.pallas_call(
        layer_kernel,
        out_shape=jax.ShapeDtypeStruct((tokens, width), bf16),
        in_specs=[pl.BlockSpec(memory_space=pltpu.VMEM)] * 7
        + [pl.BlockSpec(memory_space=pl.ANY)] * 3,
        out_specs=pl.BlockSpec(memory_space=pltpu.VMEM),
        scratch_shapes=[
            pltpu.VMEM((n_seq, 2, tokens // 2, kv.shape[1]), bf16),
            pltpu.VMEM((n_seq, 2, tokens // 2, table.shape[1]), bf16),
            pltpu.VMEM((queries.shape[0], 1), f32),
            pltpu.VMEM((queries.shape[0], 1), f32),
            pltpu.VMEM((queries.shape[0], lanes), f32),
            pltpu.VMEM((tokens, width), bf16),
            pltpu.VMEM((n_tp, block, width), bf16),
            pltpu.VMEM((block, width), bf16),
            pltpu.VMEM((block, width), bf16),
            pltpu.SemaphoreType.DMA((n_seq, 2)),
            pltpu.SemaphoreType.DMA((n_seq, 2)),
            pltpu.SemaphoreType.DMA((n_tp,)),
            pltpu.VMEM((n_seq, n_tp, block, width), bf16),
            pltpu.VMEM((slots, width, 2 * units), bf16),
            pltpu.VMEM((slots * units, width), bf16),
            pltpu.VMEM((tokens, slots * units), bf16),
            pltpu.VMEM((n_seq, n_tp, block, width), bf16),
            pltpu.VMEM((n_seq // 2, n_tp, block, width), bf16),
            pltpu.VMEM((2, n_tp, block, width), bf16),
            pltpu.VMEM((n_tp, block, width), bf16),
            pltpu.VMEM((n_tp, block, width), bf16),
            pltpu.SemaphoreType.DMA((2 * slots + 1,)),
            pltpu.SemaphoreType.DMA((112,)),
            pltpu.SemaphoreType.DMA((n_seq, n_tp)),
            pltpu.SemaphoreType.DMA((n_seq // 2,)),
            pltpu.SemaphoreType.DMA((2, n_tp)),
            pltpu.SemaphoreType.DMA((n_tp,)),
            pltpu.SemaphoreType.DMA((n_tp,)),
            pltpu.SemaphoreType.DMA((n_tp,)),
        ],
        compiler_params=pltpu.CompilerParams(
            collective_id=0, has_side_effects=True, vmem_limit_bytes=48 * 1024 * 1024
        ),
        cost_estimate=pl.CostEstimate(
            flops=flops, bytes_accessed=4 * 1024 * 1024, transcendentals=0
        ),
        name="layer",
    )(
        queries,
        kv,
        table,
        starts,
        hidden,
        norm_moe,
        w_out,
        w_gate,
        w_up,
        w_down.reshape(slots * units, width),
    )


def per_device(
    hidden,
    segment_ids,
    routes,
    gates,
    norm_attn,
    norm_moe,
    w_query,
    w_key,
    w_value,
    w_out,
    w_gate,
    w_up,
    w_down,
):
    tokens, width = hidden.shape
    queries, key_rot, value_proj, kv_cache, own_segs, query_index, starts = attention_inputs(
        hidden, segment_ids, norm_attn, w_query, w_key, w_value
    )
    table = expert_gates(routes, gates, EXPERTS)
    high = table.astype(jnp.bfloat16)
    low = (table - high.astype(jnp.float32)).astype(jnp.bfloat16)
    fill = jnp.zeros((tokens, 128 - 2 * EXPERTS), jnp.bfloat16)
    table = jnp.concatenate([high, low, fill], axis=1)
    kv_heads = key_rot.shape[1] // HEAD_DIM
    group_size = queries.shape[1] // kv_heads
    same = jnp.eye(kv_heads, dtype=jnp.bool_)
    queries = queries.transpose(1, 0, 2).reshape(kv_heads, group_size, tokens, 1, HEAD_DIM)
    queries = jnp.where(same[:, None, None, :, None], queries, 0).reshape(
        kv_heads * group_size * tokens, kv_heads * HEAD_DIM
    )
    out_rows = w_out.reshape(kv_heads, group_size, 1, HEAD_DIM, width)
    out_rows = jnp.where(same[:, None, :, None, None], out_rows, 0).reshape(
        kv_heads * group_size * kv_heads * HEAD_DIM, width
    )
    kv = jnp.concatenate([key_rot, value_proj], axis=1)
    hidden_out = run_layer(
        queries,
        kv,
        table,
        starts[:, None],
        hidden,
        norm_moe[None, :],
        out_rows,
        w_gate,
        w_up,
        w_down,
    )
    return hidden_out, kv_cache


def solution(mesh):
    whole_rows = mesh.shape["seq"] == 8 and mesh.shape["tp"] == 4
    return jax.shard_map(
        per_device if whole_rows else per_device_routed,
        mesh=mesh,
        in_specs=(
            P("seq", None),
            P(),
            P("seq", None),
            P("seq", None),
            P(),
            P(),
            P(None, "tp"),
            P(None, "tp"),
            P(None, "tp"),
            P("tp", None),
            P("seq", None, "tp"),
            P("seq", None, "tp"),
            P("seq", "tp", None),
        ),
        out_specs=(P("seq", None), P("seq", None, "tp")),
        check_vma=False,
    )
```

```python
import jax
import jax.numpy as jnp
from jax import lax
from jax.experimental import pallas as pl
from jax.experimental.pallas import tpu as pltpu
from jax.sharding import PartitionSpec as P

HEAD_DIM = 64
EXPERTS = 32


EPS = 1e-06
SCORE_SCALE = 0.015625


def normalize(values, gain):
    widened = values.astype(jnp.float32)
    return (
        widened
        * lax.rsqrt(jnp.mean(widened * widened, axis=-1, keepdims=True) + EPS)
        * gain.astype(jnp.float32)
    )


def rotary(tensor, positions):
    half_dim = tensor.shape[-1] // 2
    frequencies = 10000.0 ** (-jnp.arange(half_dim, dtype=jnp.float32) * 2.0 / tensor.shape[-1])
    angles = positions.astype(jnp.float32)[:, None] * frequencies[None, :]
    cosine = jnp.cos(angles)[:, None, :]
    sine_part = jnp.sin(angles)[:, None, :]
    lower_half = tensor[..., :half_dim]
    upper_half = tensor[..., half_dim:]
    return jnp.concatenate(
        [
            lower_half * cosine - upper_half * sine_part,
            upper_half * cosine + lower_half * sine_part,
        ],
        axis=-1,
    )


def segment_positions(segment_ids):
    index_all = jnp.arange(segment_ids.shape[0], dtype=jnp.int32)
    changed = jnp.concatenate([jnp.ones((1,), jnp.bool_), segment_ids[1:] != segment_ids[:-1]])
    starts = lax.cummax(jnp.where(changed, index_all, 0), axis=0)
    return index_all - starts


def per_device_routed(
    hidden,
    segment_ids,
    routes,
    gates,
    norm_attn,
    norm_moe,
    w_query,
    w_key,
    w_value,
    w_out,
    w_gate,
    w_up,
    w_down,
):
    tokens = hidden.shape[0]
    model_width = hidden.shape[1]
    first_row = lax.axis_index("seq") * tokens
    positions = lax.dynamic_slice_in_dim(segment_positions(segment_ids), first_row, tokens)
    own_segs = lax.dynamic_slice_in_dim(segment_ids, first_row, tokens)
    normed = normalize(hidden, norm_attn).astype(jnp.bfloat16)
    query_heads = w_query.shape[1] // HEAD_DIM
    kv_heads = w_key.shape[1] // HEAD_DIM
    group_size = query_heads // kv_heads
    queries = jnp.dot(normed, w_query, preferred_element_type=jnp.float32).reshape(
        tokens, query_heads, HEAD_DIM
    )
    queries = (
        rotary(queries, positions)
        .astype(jnp.bfloat16)
        .reshape(tokens, kv_heads, group_size, HEAD_DIM)
    )
    key_raw = jnp.dot(normed, w_key, preferred_element_type=jnp.float32).reshape(
        tokens, kv_heads, HEAD_DIM
    )
    value_proj = jnp.dot(normed, w_value, preferred_element_type=jnp.float32).astype(jnp.bfloat16)
    kv_cache = jnp.stack(
        [key_raw.reshape(tokens, kv_heads * HEAD_DIM).astype(jnp.bfloat16), value_proj], axis=1
    )
    key_rot = rotary(key_raw, positions).astype(jnp.bfloat16)
    value_heads = value_proj.reshape(tokens, kv_heads, HEAD_DIM)
    query_index = first_row + jnp.arange(tokens, dtype=jnp.int32)
    last_query = first_row + tokens - 1
    lowest_seg = own_segs[0]

    def attend(carried, key_rows, value_rows, key_start, key_segs):
        running_max, weight_sum, accumulated = carried
        scores = (
            jnp.einsum("tkgd,skd->kgts", queries, key_rows, preferred_element_type=jnp.float32)
            * SCORE_SCALE
        )
        key_index = key_start + jnp.arange(key_rows.shape[0], dtype=jnp.int32)
        allowed = (own_segs[:, None] == key_segs[None, :]) & (
            query_index[:, None] >= key_index[None, :]
        )
        masked = jnp.where(allowed, scores, -1e30)
        new_max = jnp.maximum(running_max, jnp.max(masked, axis=-1))
        weights = jnp.where(allowed, jnp.exp(masked - new_max[..., None]), 0.0)
        factor = jnp.exp(running_max - new_max)
        weight_sum = weight_sum * factor + jnp.sum(weights, axis=-1)
        accumulated = accumulated * factor[..., None] + jnp.einsum(
            "kgts,skd->kgtd",
            weights.astype(jnp.bfloat16),
            value_rows,
            preferred_element_type=jnp.float32,
        )
        return (new_max, weight_sum, accumulated)

    start_state = (
        jnp.full((kv_heads, group_size, tokens), -1e30, jnp.float32),
        jnp.zeros((kv_heads, group_size, tokens), jnp.float32),
        jnp.zeros((kv_heads, group_size, tokens, HEAD_DIM), jnp.float32),
    )
    keys_all = lax.all_gather(key_rot, "seq", axis=0, tiled=True)
    values_all = lax.all_gather(value_heads, "seq", axis=0, tiled=True)
    block_total = keys_all.shape[0] // tokens

    def visit_block(block_index, state_now):
        key_start = block_index * tokens
        key_rows = lax.dynamic_slice_in_dim(keys_all, block_index * tokens, tokens)
        value_rows = lax.dynamic_slice_in_dim(values_all, block_index * tokens, tokens)
        key_segs = lax.dynamic_slice_in_dim(segment_ids, key_start, tokens)
        relevant = (key_start <= last_query) & (key_segs[tokens - 1] >= lowest_seg)
        return lax.cond(
            relevant,
            lambda inner: attend(inner, key_rows, value_rows, key_start, key_segs),
            lambda inner: inner,
            state_now,
        )

    running_max, weight_sum, accumulated = lax.fori_loop(0, block_total, visit_block, start_state)
    attended = (
        (accumulated / weight_sum[..., None])
        .transpose(2, 0, 1, 3)
        .reshape(tokens, query_heads * HEAD_DIM)
    )
    attended = attended.astype(jnp.bfloat16)
    partial_out = jnp.dot(attended, w_out, preferred_element_type=jnp.float32)
    attn_mixed = lax.psum(partial_out.astype(jnp.bfloat16), "tp").astype(jnp.float32)
    residual = (hidden.astype(jnp.float32) + attn_mixed).astype(jnp.bfloat16)
    normed_moe = normalize(residual, norm_moe).astype(jnp.bfloat16)
    route_count = routes.shape[1]
    slots_dev = w_gate.shape[0]
    seq_count = lax.axis_size("seq")
    slot_total = slots_dev * seq_count
    copies = slot_total // EXPERTS
    block_rows = tokens // copies
    capacity = 2 * block_rows * route_count // EXPERTS
    copy_of = (jnp.arange(tokens, dtype=jnp.int32) // block_rows)[:, None]
    slot_of = routes + EXPERTS * copy_of
    flat_expert = routes.reshape(copies, block_rows * route_count)
    onehot = (
        flat_expert[:, :, None] == jnp.arange(EXPERTS, dtype=jnp.int32)[None, None, :]
    ).astype(jnp.int32)
    before = jnp.cumsum(onehot, axis=1) - onehot
    slot_rank = jnp.sum(before * onehot, axis=2).reshape(tokens, route_count)
    target = slot_of * capacity + slot_rank
    token_ids = jnp.broadcast_to(
        jnp.arange(tokens, dtype=jnp.int32)[:, None], (tokens, route_count)
    )
    source = (
        jnp.full((slot_total * capacity,), tokens, jnp.int32)
        .at[target.reshape(-1)]
        .set(token_ids.reshape(-1))
    )
    padded_rows = jnp.concatenate([normed_moe, jnp.zeros((1, normed_moe.shape[1]), jnp.bfloat16)])
    outbound = padded_rows[source].reshape(seq_count, slots_dev, capacity, normed_moe.shape[1])
    arrived = lax.all_to_all(outbound, "seq", split_axis=0, concat_axis=0, tiled=True)
    gate_val = jnp.einsum("jsrd,sdf->jsrf", arrived, w_gate, preferred_element_type=jnp.float32)
    up_val = jnp.einsum("jsrd,sdf->jsrf", arrived, w_up, preferred_element_type=jnp.float32)
    activated = (jax.nn.silu(gate_val) * up_val).astype(jnp.bfloat16)
    group_part = jnp.einsum("jsrf,sfd->jsrd", activated, w_down, preferred_element_type=jnp.float32)
    result = group_part.astype(jnp.bfloat16)
    returned = lax.all_to_all(result, "seq", split_axis=0, concat_axis=0, tiled=True).reshape(
        slot_total * capacity, model_width
    )
    picked = returned[target]
    combined = jnp.einsum(
        "tk,tkd->td",
        gates,
        picked,
        preferred_element_type=jnp.float32,
        precision=lax.Precision.HIGHEST,
    )
    expert_sum = lax.psum(combined.astype(jnp.bfloat16), "tp").astype(jnp.float32)
    hidden_out = (residual.astype(jnp.float32) + expert_sum).astype(jnp.bfloat16)
    return (hidden_out, kv_cache)


def attention_inputs(hidden, segment_ids, norm_attn, w_query, w_key, w_value):
    tokens = hidden.shape[0]
    first_row = lax.axis_index("seq") * tokens
    own_segs = lax.dynamic_slice_in_dim(segment_ids, first_row, tokens)
    query_index = first_row + jnp.arange(tokens, dtype=jnp.int32)
    starts = jnp.sum((segment_ids[None, :] < own_segs[:, None]).astype(jnp.int32), axis=1)
    positions = query_index - starts
    normed = normalize(hidden, norm_attn).astype(jnp.bfloat16)
    query_heads = w_query.shape[1] // HEAD_DIM
    kv_heads = w_key.shape[1] // HEAD_DIM
    queries = jnp.dot(normed, w_query, preferred_element_type=jnp.float32)
    key_raw = jnp.dot(normed, w_key, preferred_element_type=jnp.float32)
    value_proj = jnp.dot(normed, w_value, preferred_element_type=jnp.float32).astype(jnp.bfloat16)
    kv_cache = jnp.stack([key_raw.astype(jnp.bfloat16), value_proj], axis=1)
    queries = rotary(queries.reshape(tokens, query_heads, HEAD_DIM), positions)
    key_rot = rotary(key_raw.reshape(tokens, kv_heads, HEAD_DIM), positions)
    queries = queries.astype(jnp.bfloat16)
    key_rot = key_rot.astype(jnp.bfloat16).reshape(tokens, kv_heads * HEAD_DIM)
    return queries, key_rot, value_proj, kv_cache, own_segs, query_index, starts


def expert_gates(routes, gates, experts):
    hit = routes[:, :, None] == jnp.arange(experts, dtype=jnp.int32)[None, None, :]
    return jnp.sum(jnp.where(hit, gates[:, :, None], 0.0), axis=1)


def normalize_rows(values, gain):
    widened = values.astype(jnp.float32)
    mean = jnp.mean(widened * widened, axis=-1, keepdims=True)
    return widened * lax.rsqrt(mean + EPS) * gain.astype(jnp.float32)


def flip(seq_index, mask):
    bits = [seq_index // 4, (seq_index // 2) % 2, seq_index % 2]
    bits = [1 - bit if (mask >> (2 - n)) & 1 else bit for n, bit in enumerate(bits)]
    return bits[0] * 4 + bits[1] * 2 + bits[2]


CORE, XDIR, YDIR = 1, 2, 4


def layer_kernel(
    query_ref, kv_ref, table_ref, starts_ref, hidden_ref, norm_ref, wo_ref,
    wg_hbm, wu_hbm, wd_hbm, out_ref,
    kv, table, top, mixed, wo_all, own_heads, from_heads, residual,
    kv_sem, table_sem, wo_sem, heads_sem,
    rows, weights, downs, act, parts, from_core, first, second, from_tp,
    weight_sem, send_sem, row_sem, core_sem, first_sem, second_sem, tp_sem, out_sem,
):
    me, tp = lax.axis_index("seq"), lax.axis_index("tp")
    n_tp = rows.shape[1]
    block = rows.shape[2]
    slots = weights.shape[0]
    units = weights.shape[2] // 2
    width = rows.shape[3]
    seq_peer = {mask: (flip(me, mask), tp) for mask in (CORE, XDIR, YDIR)}
    tp_peer = {k: (me, (tp + k) % n_tp) for k in range(1, n_tp)}

    loads = []
    for n in range(slots):
        for half, source in ((0, wg_hbm), (1, wu_hbm)):
            loads.append(
                pltpu.make_async_copy(
                    source.at[n],
                    weights.at[n, :, pl.ds(half * units, units)],
                    weight_sem.at[2 * n + half],
                )
            )
    loads.append(pltpu.make_async_copy(wd_hbm, downs, weight_sem.at[2 * slots]))
    for load in loads:
        load.start()

    barrier = pltpu.get_barrier_semaphore()
    peers = list(seq_peer.values()) + list(tp_peer.values())
    for peer in peers:
        pl.semaphore_signal(
            barrier, inc=1, device_id=peer, device_id_type=pl.DeviceIdType.MESH
        )
    pl.semaphore_wait(barrier, len(peers))

    sent = []

    def send(source, target, sem, peer):
        copy = pltpu.make_async_remote_copy(
            src_ref=source,
            dst_ref=target,
            send_sem=send_sem.at[len(sent)],
            recv_sem=sem,
            device_id=peer,
            device_id_type=pl.DeviceIdType.MESH,
        )
        copy.start()
        sent.append(copy)

    def arrived(target, sem):
        pltpu.make_async_remote_copy(
            src_ref=target,
            dst_ref=target,
            send_sem=send_sem.at[0],
            recv_sem=sem,
            device_id=seq_peer[CORE],
            device_id_type=pl.DeviceIdType.MESH,
        ).wait_recv()

    def spread(buffer, sems, parts_of, place=None):
        def go(mask, k, way):
            if place is None:
                source, target = buffer.at[mask, k], buffer.at[mask ^ way, k]
            else:
                source = target = buffer.at[place(mask, k)]
            send(source, target, sems.at[mask ^ way, k], seq_peer[way])

        def take(mask, k):
            arrived(buffer.at[(mask, k) if place is None else place(mask, k)], sems.at[mask, k])

        def sides(k):
            take(XDIR, k)
            if k >= parts_of // 2:
                go(XDIR, k, YDIR)
            take(YDIR, k)
            if k < parts_of // 2:
                go(YDIR, k, XDIR)
            go(XDIR, k, CORE)
            go(YDIR, k, CORE)

        return go, take, sides

    halves = (0, 1)
    kv_go, kv_take, kv_sides = spread(kv, kv_sem, 2)
    table_go, table_take, table_sides = spread(table, table_sem, 2)
    half = kv.shape[2]
    for k in halves:
        kv[0, k] = kv_ref[k * half : (k + 1) * half, :]
        table[0, k] = table_ref[k * half : (k + 1) * half, :]
    for k in halves:
        for way in (XDIR, YDIR, CORE):
            kv_go(0, k, way)

    share = wo_ref.shape[0] // kv.shape[0]

    def wo_place(mask, k):
        start = ((tp + k) % n_tp) * wo_ref.shape[0] + flip(me, mask) * share
        return pl.ds(pl.multiple_of(start, share), share)

    wo_go, wo_take, wo_sides = spread(wo_all, wo_sem, n_tp, wo_place)
    wo_own = wo_all.at[wo_place(0, 0)]
    wo_own[...] = wo_ref[pl.ds(pl.multiple_of(me * share, share), share), :]
    for k in (2, 1, 3):
        send(wo_own, wo_own, wo_sem.at[0, n_tp - k], tp_peer[k])
    for way in (XDIR, YDIR, CORE):
        wo_go(0, 0, way)
    for k in halves:
        for way in (XDIR, YDIR, CORE):
            table_go(0, k, way)

    tokens = 2 * half
    kv_width = kv.shape[3] // 2
    heads = query_ref.shape[0] // tokens
    top[...] = jnp.full(top.shape, -3e38, jnp.float32)
    mixed[...] = jnp.zeros(mixed.shape, jnp.float32)

    def attend(masks):
        count = len(masks) * tokens
        blocks = [kv[mask].reshape(tokens, 2 * kv_width) for mask in masks]
        keys = jnp.concatenate([one[:, :kv_width] for one in blocks], axis=0)
        values = jnp.concatenate([one[:, kv_width:] for one in blocks], axis=0)
        values = jnp.concatenate([values, jnp.ones_like(values)], axis=1)
        query_index = me * tokens + lax.broadcasted_iota(jnp.int32, (tokens, tokens), 0)
        local = lax.broadcasted_iota(jnp.int32, (tokens, tokens), 1)
        allowed = []
        for mask in masks:
            key_index = flip(me, mask) * tokens + local
            allowed.append((key_index <= query_index) & (key_index >= starts_ref[...]))

        for head in range(heads):
            span = pl.ds(head * tokens, tokens)
            scores = lax.dot_general(
                query_ref[span, :],
                keys,
                (((1,), (1,)), ((), ())),
                preferred_element_type=jnp.float32,
            )
            masked = [
                jnp.where(ok, scores[:, n * tokens : (n + 1) * tokens], -3e38)
                for n, ok in enumerate(allowed)
            ]
            highest = masked[0]
            for one in masked[1:]:
                highest = jnp.maximum(highest, one)
            old_top = top[span, :]
            new_top = jnp.maximum(old_top, jnp.max(highest, axis=1, keepdims=True))
            factor = jnp.exp(old_top - new_top)
            top[span, :] = new_top
            weights_now = jnp.concatenate(
                [jnp.exp(one - new_top).astype(jnp.bfloat16) for one in masked], axis=1
            )
            mixed[span, :] = mixed[span, :] * factor + jnp.dot(
                weights_now, values, preferred_element_type=jnp.float32
            )

    diagonal = XDIR + YDIR
    attend((0,))
    for k in halves:
        kv_sides(k)
    for k in (1, 3, 2):
        wo_take(0, k)
        for way in (XDIR, YDIR, CORE):
            wo_go(0, k, way)
    for k in halves:
        kv_take(CORE, k)
    attend((CORE, XDIR, YDIR))
    for k in halves:
        kv_take(diagonal, k)
        kv_go(diagonal, k, CORE)
    for k in range(n_tp):
        wo_sides(k)
    for k in halves:
        table_sides(k)
    for mask in (XDIR + CORE, YDIR + CORE):
        for k in halves:
            kv_take(mask, k)
    attend((XDIR + CORE, YDIR + CORE))
    for k in range(n_tp):
        wo_take(diagonal, k)
        wo_go(diagonal, k, CORE)
    for k in halves:
        table_take(diagonal, k)
        table_go(diagonal, k, CORE)
    for k in halves:
        kv_take(diagonal + CORE, k)
    attend((diagonal, diagonal + CORE))

    lane_head = lax.broadcasted_iota(jnp.int32, (tokens, kv_width), 1) // HEAD_DIM
    kv_heads = kv_width // HEAD_DIM
    group_size = heads // kv_heads
    for g in range(group_size):
        joined = jnp.zeros((tokens, kv_width), jnp.float32)
        for j in range(kv_heads):
            span = pl.ds((j * group_size + g) * tokens, tokens)
            ratio = mixed[span, :kv_width] / mixed[span, kv_width:]
            joined = jnp.where(lane_head == j, ratio, joined)
        own_heads[:, g * kv_width : (g + 1) * kv_width] = joined.astype(jnp.bfloat16)

    def block_rows(k):
        return pl.ds(pl.multiple_of(((tp + k) % n_tp) * block, block), block)

    for k in (2, 1, 3):
        back = n_tp - k
        send(own_heads.at[block_rows(k)], from_heads.at[back], heads_sem.at[back], tp_peer[k])
    for mask in (CORE, XDIR + CORE, YDIR + CORE, diagonal + CORE):
        for k in range(n_tp):
            wo_take(mask, k)

    def project(block_heads, k):
        depth = wo_ref.shape[0]
        start = pl.multiple_of(((tp + k) % n_tp) * depth, depth)
        return jnp.dot(
            block_heads, wo_all[pl.ds(start, depth), :], preferred_element_type=jnp.float32
        )

    summed = project(own_heads[block_rows(0), :], 0)
    for k in (1, 3, 2):
        arrived(from_heads.at[k], heads_sem.at[k])
        summed = summed + project(from_heads[k], k)
    added = hidden_ref[block_rows(0), :].astype(jnp.float32) + summed
    residual[...] = added.astype(jnp.bfloat16)

    pass_on, take, handle_sides = spread(rows, row_sem, n_tp)
    rows[0, 0] = normalize_rows(residual[...], norm_ref[...]).astype(jnp.bfloat16)
    for k in (2, 1, 3):
        back = n_tp - k
        send(rows.at[0, 0], rows.at[0, back], row_sem.at[0, back], tp_peer[k])
    for way in (XDIR, YDIR, CORE):
        pass_on(0, 0, way)
    for mask in (CORE, XDIR + CORE, YDIR + CORE, XDIR + YDIR + CORE):
        for k in halves:
            table_take(mask, k)

    def compute(mask):
        group = rows[mask].reshape(n_tp * block, width)
        gate = jnp.concatenate(
            [
                table[
                    mask,
                    ((tp + k) % n_tp) // 2,
                    pl.ds(pl.multiple_of(((tp + k) % 2) * block, block), block),
                    :,
                ]
                for k in range(n_tp)
            ],
            axis=0,
        ).astype(jnp.float32)
        lane = lax.broadcasted_iota(jnp.int32, gate.shape, 1)
        for n in range(slots):
            both = jnp.dot(group, weights[n], preferred_element_type=jnp.float32)
            gate_val, up_val = both[:, :units], both[:, units:]
            column = me * slots + n
            chosen = (lane == column) | (lane == column + EXPERTS)
            scale = jnp.sum(jnp.where(chosen, gate, 0.0), axis=1, keepdims=True)
            value = gate_val / (1.0 + jnp.exp(-gate_val)) * up_val * scale
            act[:, n * units : (n + 1) * units] = jnp.where(scale > 0, value, 0.0).astype(
                jnp.bfloat16
            )
        step = 256
        for column in range(0, width, step):
            piece = jnp.dot(
                act[...],
                downs[:, column : column + step],
                preferred_element_type=jnp.float32,
            ).astype(jnp.bfloat16)
            for k in range(n_tp):
                parts[mask, k, :, column : column + step] = piece[k * block : (k + 1) * block]

    def give_core(mask):
        send(parts.at[mask], from_core.at[mask // 2], core_sem.at[mask // 2], seq_peer[CORE])

    def add(mask, k, extra):
        parts[mask, k] = (
            parts[mask, k].astype(jnp.float32) + extra.astype(jnp.float32)
        ).astype(jnp.bfloat16)

    def add_core(mask):
        arrived(from_core.at[mask // 2], core_sem.at[mask // 2])
        for k in range(n_tp):
            add(mask, k, from_core[mask // 2, k])

    for k in (1, 3, 2):
        take(0, k)
        for way in (XDIR, YDIR, CORE):
            pass_on(0, k, way)
    handle_sides(0)
    handle_sides(1)
    for load in loads:
        load.wait()
    compute(0)
    handle_sides(3)
    handle_sides(2)
    for k in range(n_tp):
        take(CORE, k)
    compute(1)
    give_core(1)
    compute(2)
    compute(4)
    for mask in (XDIR + CORE, YDIR + CORE):
        for k in range(n_tp):
            take(mask, k)
        compute(mask)
        give_core(mask)
    for k in range(n_tp):
        take(diagonal, k)
        pass_on(diagonal, k, CORE)
    compute(diagonal)
    for k in range(n_tp):
        take(diagonal + CORE, k)
    compute(diagonal + CORE)
    give_core(diagonal + CORE)

    early = ((XDIR, YDIR, (1, 0)), (YDIR, XDIR, (2, 3)))

    def give_first(mask, way, ks):
        for k in ks:
            slot = 0 if mask == way else 1
            send(parts.at[mask, k], first.at[slot, k], first_sem.at[slot, k], seq_peer[way])

    for way, other, ks in early:
        add_core(way)
        give_first(way, way, ks)
    add_core(XDIR + YDIR)
    for way, other, ks in early:
        give_first(XDIR + YDIR, way, ks)
    add_core(0)
    for other, k in ((YDIR, 1), (XDIR, 2), (YDIR, 0), (XDIR, 3)):
        arrived(first.at[1, k], first_sem.at[1, k])
        add(other, k, first[1, k])
        send(parts.at[other, k], second.at[k], second_sem.at[k], seq_peer[other])
    for k in (2, 1, 3, 0):
        arrived(first.at[0, k], first_sem.at[0, k])
        add(0, k, first[0, k])
    for k in (2, 1, 3, 0):
        arrived(second.at[k], second_sem.at[k])
        add(0, k, second[k])
        if k:
            back = n_tp - k
            send(parts.at[0, k], from_tp.at[back], tp_sem.at[back], tp_peer[k])
    total = residual[...].astype(jnp.float32) + parts[0, 0].astype(jnp.float32)
    for k in (1, 3, 2):
        arrived(from_tp.at[k], tp_sem.at[k])
        total = total + from_tp[k].astype(jnp.float32)
    own = out_ref.at[pl.ds(pl.multiple_of(tp * block, block), block)]
    own[...] = total.astype(jnp.bfloat16)
    for k in (2, 1, 3):
        send(own, own, out_sem.at[n_tp - k], tp_peer[k])
    for k in (1, 3, 2):
        start = pl.multiple_of(((tp + k) % n_tp) * block, block)
        arrived(out_ref.at[pl.ds(start, block)], out_sem.at[k])
    for copy in sent:
        copy.wait_send()


def run_layer(queries, kv, table, starts, hidden, norm_moe, w_out, w_gate, w_up, w_down):
    tokens, width = hidden.shape
    n_tp = lax.axis_size("tp")
    n_seq = lax.axis_size("seq")
    block = tokens // n_tp
    slots, _, units = w_gate.shape
    lanes = queries.shape[1]
    bf16, f32 = jnp.bfloat16, jnp.float32
    flops = 2 * n_seq * tokens * slots * width * units * 3
    return pl.pallas_call(
        layer_kernel,
        out_shape=jax.ShapeDtypeStruct((tokens, width), bf16),
        in_specs=[pl.BlockSpec(memory_space=pltpu.VMEM)] * 7
        + [pl.BlockSpec(memory_space=pl.ANY)] * 3,
        out_specs=pl.BlockSpec(memory_space=pltpu.VMEM),
        scratch_shapes=[
            pltpu.VMEM((n_seq, 2, tokens // 2, kv.shape[1]), bf16),
            pltpu.VMEM((n_seq, 2, tokens // 2, table.shape[1]), bf16),
            pltpu.VMEM((queries.shape[0], 1), f32),
            pltpu.VMEM((queries.shape[0], 2 * lanes), f32),
            pltpu.VMEM((n_tp * w_out.shape[0], width), bf16),
            pltpu.VMEM((tokens, w_out.shape[0]), bf16),
            pltpu.VMEM((n_tp, block, w_out.shape[0]), bf16),
            pltpu.VMEM((block, width), bf16),
            pltpu.SemaphoreType.DMA((n_seq, 2)),
            pltpu.SemaphoreType.DMA((n_seq, 2)),
            pltpu.SemaphoreType.DMA((n_seq, n_tp)),
            pltpu.SemaphoreType.DMA((n_tp,)),
            pltpu.VMEM((n_seq, n_tp, block, width), bf16),
            pltpu.VMEM((slots, width, 2 * units), bf16),
            pltpu.VMEM((slots * units, width), bf16),
            pltpu.VMEM((tokens, slots * units), bf16),
            pltpu.VMEM((n_seq, n_tp, block, width), bf16),
            pltpu.VMEM((n_seq // 2, n_tp, block, width), bf16),
            pltpu.VMEM((2, n_tp, block, width), bf16),
            pltpu.VMEM((n_tp, block, width), bf16),
            pltpu.VMEM((n_tp, block, width), bf16),
            pltpu.SemaphoreType.DMA((2 * slots + 1,)),
            pltpu.SemaphoreType.DMA((144,)),
            pltpu.SemaphoreType.DMA((n_seq, n_tp)),
            pltpu.SemaphoreType.DMA((n_seq // 2,)),
            pltpu.SemaphoreType.DMA((2, n_tp)),
            pltpu.SemaphoreType.DMA((n_tp,)),
            pltpu.SemaphoreType.DMA((n_tp,)),
            pltpu.SemaphoreType.DMA((n_tp,)),
        ],
        compiler_params=pltpu.CompilerParams(
            collective_id=0, has_side_effects=True, vmem_limit_bytes=48 * 1024 * 1024
        ),
        cost_estimate=pl.CostEstimate(
            flops=flops, bytes_accessed=4 * 1024 * 1024, transcendentals=0
        ),
        name="layer",
    )(
        queries,
        kv,
        table,
        starts,
        hidden,
        norm_moe,
        w_out,
        w_gate,
        w_up,
        w_down.reshape(slots * units, width),
    )


def per_device(
    hidden,
    segment_ids,
    routes,
    gates,
    norm_attn,
    norm_moe,
    w_query,
    w_key,
    w_value,
    w_out,
    w_gate,
    w_up,
    w_down,
):
    tokens, width = hidden.shape
    queries, key_rot, value_proj, kv_cache, own_segs, query_index, starts = attention_inputs(
        hidden, segment_ids, norm_attn, w_query, w_key, w_value
    )
    table = expert_gates(routes, gates, EXPERTS)
    high = table.astype(jnp.bfloat16)
    low = (table - high.astype(jnp.float32)).astype(jnp.bfloat16)
    fill = jnp.zeros((tokens, 128 - 2 * EXPERTS), jnp.bfloat16)
    table = jnp.concatenate([high, low, fill], axis=1)
    kv_heads = key_rot.shape[1] // HEAD_DIM
    group_size = queries.shape[1] // kv_heads
    same = jnp.eye(kv_heads, dtype=jnp.bool_)
    queries = queries.transpose(1, 0, 2).reshape(kv_heads, group_size, tokens, 1, HEAD_DIM)
    queries = jnp.where(same[:, None, None, :, None], queries * SCORE_SCALE, 0).reshape(
        kv_heads * group_size * tokens, kv_heads * HEAD_DIM
    )
    out_rows = w_out.reshape(kv_heads, group_size, HEAD_DIM, width).transpose(1, 0, 2, 3)
    out_rows = out_rows.reshape(w_out.shape)
    kv = jnp.concatenate([key_rot, value_proj], axis=1)
    hidden_out = run_layer(
        queries,
        kv,
        table,
        starts[:, None],
        hidden,
        norm_moe[None, :],
        out_rows,
        w_gate,
        w_up,
        w_down,
    )
    return hidden_out, kv_cache


def solution(mesh):
    whole_rows = mesh.shape["seq"] == 8 and mesh.shape["tp"] == 4
    return jax.shard_map(
        per_device if whole_rows else per_device_routed,
        mesh=mesh,
        in_specs=(
            P("seq", None),
            P(),
            P("seq", None),
            P("seq", None),
            P(),
            P(),
            P(None, "tp"),
            P(None, "tp"),
            P(None, "tp"),
            P("tp", None),
            P("seq", None, "tp"),
            P("seq", None, "tp"),
            P("seq", "tp", None),
        ),
        out_specs=(P("seq", None), P("seq", None, "tp")),
        check_vma=False,
    )
```

```python
import jax
import jax.numpy as jnp
from jax import lax
from jax.experimental import pallas as pl
from jax.experimental.pallas import tpu as pltpu
from jax.sharding import PartitionSpec as P

HEAD_DIM = 64
EXPERTS = 32


EPS = 1e-06
SCORE_SCALE = 0.015625


def normalize(values, gain):
    widened = values.astype(jnp.float32)
    return (
        widened
        * lax.rsqrt(jnp.mean(widened * widened, axis=-1, keepdims=True) + EPS)
        * gain.astype(jnp.float32)
    )


def rotary(tensor, positions):
    half_dim = tensor.shape[-1] // 2
    frequencies = 10000.0 ** (-jnp.arange(half_dim, dtype=jnp.float32) * 2.0 / tensor.shape[-1])
    angles = positions.astype(jnp.float32)[:, None] * frequencies[None, :]
    cosine = jnp.cos(angles)[:, None, :]
    sine_part = jnp.sin(angles)[:, None, :]
    lower_half = tensor[..., :half_dim]
    upper_half = tensor[..., half_dim:]
    return jnp.concatenate(
        [
            lower_half * cosine - upper_half * sine_part,
            upper_half * cosine + lower_half * sine_part,
        ],
        axis=-1,
    )


def segment_positions(segment_ids):
    index_all = jnp.arange(segment_ids.shape[0], dtype=jnp.int32)
    changed = jnp.concatenate([jnp.ones((1,), jnp.bool_), segment_ids[1:] != segment_ids[:-1]])
    starts = lax.cummax(jnp.where(changed, index_all, 0), axis=0)
    return index_all - starts


def per_device_routed(
    hidden,
    segment_ids,
    routes,
    gates,
    norm_attn,
    norm_moe,
    w_query,
    w_key,
    w_value,
    w_out,
    w_gate,
    w_up,
    w_down,
):
    tokens = hidden.shape[0]
    model_width = hidden.shape[1]
    first_row = lax.axis_index("seq") * tokens
    positions = lax.dynamic_slice_in_dim(segment_positions(segment_ids), first_row, tokens)
    own_segs = lax.dynamic_slice_in_dim(segment_ids, first_row, tokens)
    normed = normalize(hidden, norm_attn).astype(jnp.bfloat16)
    query_heads = w_query.shape[1] // HEAD_DIM
    kv_heads = w_key.shape[1] // HEAD_DIM
    group_size = query_heads // kv_heads
    queries = jnp.dot(normed, w_query, preferred_element_type=jnp.float32).reshape(
        tokens, query_heads, HEAD_DIM
    )
    queries = (
        rotary(queries, positions)
        .astype(jnp.bfloat16)
        .reshape(tokens, kv_heads, group_size, HEAD_DIM)
    )
    key_raw = jnp.dot(normed, w_key, preferred_element_type=jnp.float32).reshape(
        tokens, kv_heads, HEAD_DIM
    )
    value_proj = jnp.dot(normed, w_value, preferred_element_type=jnp.float32).astype(jnp.bfloat16)
    kv_cache = jnp.stack(
        [key_raw.reshape(tokens, kv_heads * HEAD_DIM).astype(jnp.bfloat16), value_proj], axis=1
    )
    key_rot = rotary(key_raw, positions).astype(jnp.bfloat16)
    value_heads = value_proj.reshape(tokens, kv_heads, HEAD_DIM)
    query_index = first_row + jnp.arange(tokens, dtype=jnp.int32)
    last_query = first_row + tokens - 1
    lowest_seg = own_segs[0]

    def attend(carried, key_rows, value_rows, key_start, key_segs):
        running_max, weight_sum, accumulated = carried
        scores = (
            jnp.einsum("tkgd,skd->kgts", queries, key_rows, preferred_element_type=jnp.float32)
            * SCORE_SCALE
        )
        key_index = key_start + jnp.arange(key_rows.shape[0], dtype=jnp.int32)
        allowed = (own_segs[:, None] == key_segs[None, :]) & (
            query_index[:, None] >= key_index[None, :]
        )
        masked = jnp.where(allowed, scores, -1e30)
        new_max = jnp.maximum(running_max, jnp.max(masked, axis=-1))
        weights = jnp.where(allowed, jnp.exp(masked - new_max[..., None]), 0.0)
        factor = jnp.exp(running_max - new_max)
        weight_sum = weight_sum * factor + jnp.sum(weights, axis=-1)
        accumulated = accumulated * factor[..., None] + jnp.einsum(
            "kgts,skd->kgtd",
            weights.astype(jnp.bfloat16),
            value_rows,
            preferred_element_type=jnp.float32,
        )
        return (new_max, weight_sum, accumulated)

    start_state = (
        jnp.full((kv_heads, group_size, tokens), -1e30, jnp.float32),
        jnp.zeros((kv_heads, group_size, tokens), jnp.float32),
        jnp.zeros((kv_heads, group_size, tokens, HEAD_DIM), jnp.float32),
    )
    keys_all = lax.all_gather(key_rot, "seq", axis=0, tiled=True)
    values_all = lax.all_gather(value_heads, "seq", axis=0, tiled=True)
    block_total = keys_all.shape[0] // tokens

    def visit_block(block_index, state_now):
        key_start = block_index * tokens
        key_rows = lax.dynamic_slice_in_dim(keys_all, block_index * tokens, tokens)
        value_rows = lax.dynamic_slice_in_dim(values_all, block_index * tokens, tokens)
        key_segs = lax.dynamic_slice_in_dim(segment_ids, key_start, tokens)
        relevant = (key_start <= last_query) & (key_segs[tokens - 1] >= lowest_seg)
        return lax.cond(
            relevant,
            lambda inner: attend(inner, key_rows, value_rows, key_start, key_segs),
            lambda inner: inner,
            state_now,
        )

    running_max, weight_sum, accumulated = lax.fori_loop(0, block_total, visit_block, start_state)
    attended = (
        (accumulated / weight_sum[..., None])
        .transpose(2, 0, 1, 3)
        .reshape(tokens, query_heads * HEAD_DIM)
    )
    attended = attended.astype(jnp.bfloat16)
    partial_out = jnp.dot(attended, w_out, preferred_element_type=jnp.float32)
    attn_mixed = lax.psum(partial_out.astype(jnp.bfloat16), "tp").astype(jnp.float32)
    residual = (hidden.astype(jnp.float32) + attn_mixed).astype(jnp.bfloat16)
    normed_moe = normalize(residual, norm_moe).astype(jnp.bfloat16)
    route_count = routes.shape[1]
    slots_dev = w_gate.shape[0]
    seq_count = lax.axis_size("seq")
    slot_total = slots_dev * seq_count
    copies = slot_total // EXPERTS
    block_rows = tokens // copies
    capacity = 2 * block_rows * route_count // EXPERTS
    copy_of = (jnp.arange(tokens, dtype=jnp.int32) // block_rows)[:, None]
    slot_of = routes + EXPERTS * copy_of
    flat_expert = routes.reshape(copies, block_rows * route_count)
    onehot = (
        flat_expert[:, :, None] == jnp.arange(EXPERTS, dtype=jnp.int32)[None, None, :]
    ).astype(jnp.int32)
    before = jnp.cumsum(onehot, axis=1) - onehot
    slot_rank = jnp.sum(before * onehot, axis=2).reshape(tokens, route_count)
    target = slot_of * capacity + slot_rank
    token_ids = jnp.broadcast_to(
        jnp.arange(tokens, dtype=jnp.int32)[:, None], (tokens, route_count)
    )
    source = (
        jnp.full((slot_total * capacity,), tokens, jnp.int32)
        .at[target.reshape(-1)]
        .set(token_ids.reshape(-1))
    )
    padded_rows = jnp.concatenate([normed_moe, jnp.zeros((1, normed_moe.shape[1]), jnp.bfloat16)])
    outbound = padded_rows[source].reshape(seq_count, slots_dev, capacity, normed_moe.shape[1])
    arrived = lax.all_to_all(outbound, "seq", split_axis=0, concat_axis=0, tiled=True)
    gate_val = jnp.einsum("jsrd,sdf->jsrf", arrived, w_gate, preferred_element_type=jnp.float32)
    up_val = jnp.einsum("jsrd,sdf->jsrf", arrived, w_up, preferred_element_type=jnp.float32)
    activated = (jax.nn.silu(gate_val) * up_val).astype(jnp.bfloat16)
    group_part = jnp.einsum("jsrf,sfd->jsrd", activated, w_down, preferred_element_type=jnp.float32)
    result = group_part.astype(jnp.bfloat16)
    returned = lax.all_to_all(result, "seq", split_axis=0, concat_axis=0, tiled=True).reshape(
        slot_total * capacity, model_width
    )
    picked = returned[target]
    combined = jnp.einsum(
        "tk,tkd->td",
        gates,
        picked,
        preferred_element_type=jnp.float32,
        precision=lax.Precision.HIGHEST,
    )
    expert_sum = lax.psum(combined.astype(jnp.bfloat16), "tp").astype(jnp.float32)
    hidden_out = (residual.astype(jnp.float32) + expert_sum).astype(jnp.bfloat16)
    return (hidden_out, kv_cache)


def attention_inputs(hidden, segment_ids, norm_attn, w_query, w_key, w_value):
    tokens = hidden.shape[0]
    first_row = lax.axis_index("seq") * tokens
    own_segs = lax.dynamic_slice_in_dim(segment_ids, first_row, tokens)
    query_index = first_row + jnp.arange(tokens, dtype=jnp.int32)
    starts = jnp.sum((segment_ids[None, :] < own_segs[:, None]).astype(jnp.int32), axis=1)
    positions = query_index - starts
    normed = normalize(hidden, norm_attn).astype(jnp.bfloat16)
    query_heads = w_query.shape[1] // HEAD_DIM
    kv_heads = w_key.shape[1] // HEAD_DIM
    queries = jnp.dot(normed, w_query, preferred_element_type=jnp.float32)
    key_raw = jnp.dot(normed, w_key, preferred_element_type=jnp.float32)
    value_proj = jnp.dot(normed, w_value, preferred_element_type=jnp.float32).astype(jnp.bfloat16)
    kv_cache = jnp.stack([key_raw.astype(jnp.bfloat16), value_proj], axis=1)
    queries = rotary(queries.reshape(tokens, query_heads, HEAD_DIM), positions)
    key_rot = rotary(key_raw.reshape(tokens, kv_heads, HEAD_DIM), positions)
    queries = queries.astype(jnp.bfloat16)
    key_rot = key_rot.astype(jnp.bfloat16).reshape(tokens, kv_heads * HEAD_DIM)
    return queries, key_rot, value_proj, kv_cache, own_segs, query_index, starts


def expert_gates(routes, gates, experts):
    hit = routes[:, :, None] == jnp.arange(experts, dtype=jnp.int32)[None, None, :]
    return jnp.sum(jnp.where(hit, gates[:, :, None], 0.0), axis=1)


def normalize_rows(values, gain):
    widened = values.astype(jnp.float32)
    mean = jnp.mean(widened * widened, axis=-1, keepdims=True)
    return widened * lax.rsqrt(mean + EPS) * gain.astype(jnp.float32)


def flip(seq_index, mask):
    bits = [seq_index // 4, (seq_index // 2) % 2, seq_index % 2]
    bits = [1 - bit if (mask >> (2 - n)) & 1 else bit for n, bit in enumerate(bits)]
    return bits[0] * 4 + bits[1] * 2 + bits[2]


CORE, XDIR, YDIR = 1, 2, 4


def layer_kernel(
    query_ref, kv_ref, table_ref, starts_ref, hidden_ref, norm_ref, wo_ref,
    wg_hbm, wu_hbm, wd_hbm, out_ref,
    kv, table, hidden_rows, top, mixed, wo_all, own_heads, from_heads, residual,
    kv_sem, table_sem, wo_sem, heads_sem,
    rows, weights, downs, act, parts, from_core, first, second, from_tp,
    weight_sem, send_sem, row_sem, core_sem, first_sem, second_sem, tp_sem, out_sem,
):
    me, tp = lax.axis_index("seq"), lax.axis_index("tp")
    n_tp = rows.shape[1]
    block = rows.shape[2]
    slots = weights.shape[0]
    units = weights.shape[2] // 2
    width = rows.shape[3]
    seq_peer = {mask: (flip(me, mask), tp) for mask in (CORE, XDIR, YDIR)}
    tp_peer = {k: (me, (tp + k) % n_tp) for k in range(1, n_tp)}

    loads = []
    for n in range(slots):
        for half, source in ((0, wg_hbm), (1, wu_hbm)):
            loads.append(
                pltpu.make_async_copy(
                    source.at[n],
                    weights.at[n, :, pl.ds(half * units, units)],
                    weight_sem.at[2 * n + half],
                )
            )
    loads.append(pltpu.make_async_copy(wd_hbm, downs, weight_sem.at[2 * slots]))
    share = wo_ref.shape[0] // kv.shape[0]
    own_share = pltpu.make_async_copy(
        wo_ref.at[pl.ds(pl.multiple_of(me * share, share), share)],
        wo_all.at[
            pl.ds(pl.multiple_of(tp * wo_ref.shape[0] + me * share, share), share)
        ],
        weight_sem.at[2 * slots + 1],
    )
    own_share.start()
    own_hidden = pltpu.make_async_copy(
        hidden_ref.at[pl.ds(pl.multiple_of(tp * block, block), block)],
        hidden_rows,
        weight_sem.at[2 * slots + 2],
    )
    own_hidden.start()
    for load in loads:
        load.start()

    barrier = pltpu.get_barrier_semaphore()
    peers = list(seq_peer.values()) + list(tp_peer.values())
    for peer in peers:
        pl.semaphore_signal(
            barrier, inc=1, device_id=peer, device_id_type=pl.DeviceIdType.MESH
        )
    pl.semaphore_wait(barrier, len(peers))

    sent = []

    def send(source, target, sem, peer):
        copy = pltpu.make_async_remote_copy(
            src_ref=source,
            dst_ref=target,
            send_sem=send_sem.at[len(sent)],
            recv_sem=sem,
            device_id=peer,
            device_id_type=pl.DeviceIdType.MESH,
        )
        copy.start()
        sent.append(copy)

    def arrived(target, sem):
        pltpu.make_async_remote_copy(
            src_ref=target,
            dst_ref=target,
            send_sem=send_sem.at[0],
            recv_sem=sem,
            device_id=seq_peer[CORE],
            device_id_type=pl.DeviceIdType.MESH,
        ).wait_recv()

    def spread(buffer, sems, parts_of, place=None):
        def go(mask, k, way):
            if place is None:
                source, target = buffer.at[mask, k], buffer.at[mask ^ way, k]
            else:
                source = target = buffer.at[place(mask, k)]
            send(source, target, sems.at[mask ^ way, k], seq_peer[way])

        def take(mask, k):
            arrived(buffer.at[(mask, k) if place is None else place(mask, k)], sems.at[mask, k])

        def sides(k):
            take(XDIR, k)
            if k >= parts_of // 2:
                go(XDIR, k, YDIR)
            take(YDIR, k)
            if k < parts_of // 2:
                go(YDIR, k, XDIR)
            go(XDIR, k, CORE)
            go(YDIR, k, CORE)

        return go, take, sides

    halves = (0, 1)
    kv_go, kv_take, kv_sides = spread(kv, kv_sem, 2)
    table_go, table_take, table_sides = spread(table, table_sem, 2)
    half = kv.shape[2]
    for k in halves:
        kv[0, k] = kv_ref[k * half : (k + 1) * half, :]
        table[0, k] = table_ref[k * half : (k + 1) * half, :]
    for k in halves:
        for way in (XDIR, YDIR, CORE):
            kv_go(0, k, way)

    def wo_place(mask, k):
        start = ((tp + k) % n_tp) * wo_ref.shape[0] + flip(me, mask) * share
        return pl.ds(pl.multiple_of(start, share), share)

    wo_go, wo_take, wo_sides = spread(wo_all, wo_sem, n_tp, wo_place)
    wo_own = wo_all.at[wo_place(0, 0)]
    own_share.wait()
    for k in (2, 1, 3):
        send(wo_own, wo_own, wo_sem.at[0, n_tp - k], tp_peer[k])
    for way in (XDIR, YDIR, CORE):
        wo_go(0, 0, way)
    for k in halves:
        for way in (XDIR, YDIR, CORE):
            table_go(0, k, way)

    tokens = 2 * half
    kv_width = kv.shape[3] // 2
    heads = query_ref.shape[0] // tokens
    top[...] = jnp.full(top.shape, -3e38, jnp.float32)
    mixed[...] = jnp.zeros(mixed.shape, jnp.float32)

    def attend(masks):
        count = len(masks) * tokens
        blocks = [kv[mask].reshape(tokens, 2 * kv_width) for mask in masks]
        keys = jnp.concatenate([one[:, :kv_width] for one in blocks], axis=0)
        values = jnp.concatenate([one[:, kv_width:] for one in blocks], axis=0)
        values = jnp.concatenate([values, jnp.ones_like(values)], axis=1)
        query_index = me * tokens + lax.broadcasted_iota(jnp.int32, (tokens, tokens), 0)
        local = lax.broadcasted_iota(jnp.int32, (tokens, tokens), 1)
        allowed = []
        for mask in masks:
            key_index = flip(me, mask) * tokens + local
            allowed.append((key_index <= query_index) & (key_index >= starts_ref[...]))

        for head in range(heads):
            span = pl.ds(head * tokens, tokens)
            scores = lax.dot_general(
                query_ref[span, :],
                keys,
                (((1,), (1,)), ((), ())),
                preferred_element_type=jnp.float32,
            )
            masked = [
                jnp.where(ok, scores[:, n * tokens : (n + 1) * tokens], -3e38)
                for n, ok in enumerate(allowed)
            ]
            highest = masked[0]
            for one in masked[1:]:
                highest = jnp.maximum(highest, one)
            old_top = top[span, :]
            new_top = jnp.maximum(old_top, jnp.max(highest, axis=1, keepdims=True))
            factor = jnp.exp(old_top - new_top)
            top[span, :] = new_top
            weights_now = jnp.concatenate(
                [jnp.exp(one - new_top).astype(jnp.bfloat16) for one in masked], axis=1
            )
            mixed[span, :] = mixed[span, :] * factor + jnp.dot(
                weights_now, values, preferred_element_type=jnp.float32
            )

    diagonal = XDIR + YDIR
    attend((0,))
    for k in halves:
        kv_sides(k)
    for k in (1, 3, 2):
        wo_take(0, k)
        for way in (XDIR, YDIR, CORE):
            wo_go(0, k, way)
    for k in halves:
        kv_take(CORE, k)
    attend((CORE, XDIR, YDIR))
    for k in halves:
        kv_take(diagonal, k)
        kv_go(diagonal, k, CORE)
    for k in range(n_tp):
        wo_sides(k)
    for k in halves:
        table_sides(k)
    for mask in (XDIR + CORE, YDIR + CORE):
        for k in halves:
            kv_take(mask, k)
    attend((XDIR + CORE, YDIR + CORE))
    for k in range(n_tp):
        wo_take(diagonal, k)
        wo_go(diagonal, k, CORE)
    for k in halves:
        table_take(diagonal, k)
        table_go(diagonal, k, CORE)
    for k in halves:
        kv_take(diagonal + CORE, k)
    attend((diagonal, diagonal + CORE))

    lane_head = lax.broadcasted_iota(jnp.int32, (tokens, kv_width), 1) // HEAD_DIM
    kv_heads = kv_width // HEAD_DIM
    group_size = heads // kv_heads
    for g in range(group_size):
        joined = jnp.zeros((tokens, kv_width), jnp.float32)
        for j in range(kv_heads):
            span = pl.ds((j * group_size + g) * tokens, tokens)
            ratio = mixed[span, :kv_width] / mixed[span, kv_width:]
            joined = jnp.where(lane_head == j, ratio, joined)
        own_heads[:, g * kv_width : (g + 1) * kv_width] = joined.astype(jnp.bfloat16)

    def block_rows(k):
        return pl.ds(pl.multiple_of(((tp + k) % n_tp) * block, block), block)

    for k in (2, 1, 3):
        back = n_tp - k
        send(own_heads.at[block_rows(k)], from_heads.at[back], heads_sem.at[back], tp_peer[k])
    for mask in (CORE, XDIR + CORE, YDIR + CORE, diagonal + CORE):
        for k in range(n_tp):
            wo_take(mask, k)

    def project(block_heads, k):
        depth = wo_ref.shape[0]
        start = pl.multiple_of(((tp + k) % n_tp) * depth, depth)
        return jnp.dot(
            block_heads, wo_all[pl.ds(start, depth), :], preferred_element_type=jnp.float32
        )

    summed = project(own_heads[block_rows(0), :], 0)
    for k in (1, 3, 2):
        arrived(from_heads.at[k], heads_sem.at[k])
        summed = summed + project(from_heads[k], k)
    own_hidden.wait()
    added = hidden_rows[...].astype(jnp.float32) + summed
    residual[...] = added.astype(jnp.bfloat16)

    pass_on, take, handle_sides = spread(rows, row_sem, n_tp)
    rows[0, 0] = normalize_rows(residual[...], norm_ref[...]).astype(jnp.bfloat16)
    for k in (2, 1, 3):
        back = n_tp - k
        send(rows.at[0, 0], rows.at[0, back], row_sem.at[0, back], tp_peer[k])
    for way in (XDIR, YDIR, CORE):
        pass_on(0, 0, way)
    for mask in (CORE, XDIR + CORE, YDIR + CORE, XDIR + YDIR + CORE):
        for k in halves:
            table_take(mask, k)

    def compute(mask):
        group = rows[mask].reshape(n_tp * block, width)
        gate = jnp.concatenate(
            [
                table[
                    mask,
                    ((tp + k) % n_tp) // 2,
                    pl.ds(pl.multiple_of(((tp + k) % 2) * block, block), block),
                    :,
                ]
                for k in range(n_tp)
            ],
            axis=0,
        ).astype(jnp.float32)
        lane = lax.broadcasted_iota(jnp.int32, gate.shape, 1)
        for n in range(slots):
            both = jnp.dot(group, weights[n], preferred_element_type=jnp.float32)
            gate_val, up_val = both[:, :units], both[:, units:]
            column = me * slots + n
            chosen = (lane == column) | (lane == column + EXPERTS)
            scale = jnp.sum(jnp.where(chosen, gate, 0.0), axis=1, keepdims=True)
            value = gate_val / (1.0 + jnp.exp(-gate_val)) * up_val * scale
            act[:, n * units : (n + 1) * units] = jnp.where(scale > 0, value, 0.0).astype(
                jnp.bfloat16
            )
        step = 256
        for column in range(0, width, step):
            piece = jnp.dot(
                act[...],
                downs[:, column : column + step],
                preferred_element_type=jnp.float32,
            ).astype(jnp.bfloat16)
            for k in range(n_tp):
                parts[mask, k, :, column : column + step] = piece[k * block : (k + 1) * block]

    def give_core(mask):
        send(parts.at[mask], from_core.at[mask // 2], core_sem.at[mask // 2], seq_peer[CORE])

    def add(mask, k, extra):
        parts[mask, k] = (
            parts[mask, k].astype(jnp.float32) + extra.astype(jnp.float32)
        ).astype(jnp.bfloat16)

    def add_core(mask):
        arrived(from_core.at[mask // 2], core_sem.at[mask // 2])
        for k in range(n_tp):
            add(mask, k, from_core[mask // 2, k])

    for k in (1, 3, 2):
        take(0, k)
        for way in (XDIR, YDIR, CORE):
            pass_on(0, k, way)
    handle_sides(0)
    handle_sides(1)
    for load in loads:
        load.wait()
    compute(0)
    handle_sides(3)
    handle_sides(2)
    for k in range(n_tp):
        take(CORE, k)
    compute(1)
    give_core(1)
    compute(2)
    compute(4)
    for mask in (XDIR + CORE, YDIR + CORE):
        for k in range(n_tp):
            take(mask, k)
        compute(mask)
        give_core(mask)
    for k in range(n_tp):
        take(diagonal, k)
        pass_on(diagonal, k, CORE)
    compute(diagonal)
    for k in range(n_tp):
        take(diagonal + CORE, k)
    compute(diagonal + CORE)
    give_core(diagonal + CORE)

    early = ((XDIR, YDIR, (1, 0)), (YDIR, XDIR, (2, 3)))

    def give_first(mask, way, ks):
        for k in ks:
            slot = 0 if mask == way else 1
            send(parts.at[mask, k], first.at[slot, k], first_sem.at[slot, k], seq_peer[way])

    for way, other, ks in early:
        add_core(way)
        give_first(way, way, ks)
    add_core(XDIR + YDIR)
    for way, other, ks in early:
        give_first(XDIR + YDIR, way, ks)
    add_core(0)
    for other, k in ((YDIR, 1), (XDIR, 2), (YDIR, 0), (XDIR, 3)):
        arrived(first.at[1, k], first_sem.at[1, k])
        add(other, k, first[1, k])
        send(parts.at[other, k], second.at[k], second_sem.at[k], seq_peer[other])
    for k in (2, 1, 3, 0):
        arrived(first.at[0, k], first_sem.at[0, k])
        add(0, k, first[0, k])
    for k in (2, 1, 3, 0):
        arrived(second.at[k], second_sem.at[k])
        add(0, k, second[k])
        if k:
            back = n_tp - k
            send(parts.at[0, k], from_tp.at[back], tp_sem.at[back], tp_peer[k])
    total = residual[...].astype(jnp.float32) + parts[0, 0].astype(jnp.float32)
    for k in (1, 3, 2):
        arrived(from_tp.at[k], tp_sem.at[k])
        total = total + from_tp[k].astype(jnp.float32)
    own = out_ref.at[pl.ds(pl.multiple_of(tp * block, block), block)]
    own[...] = total.astype(jnp.bfloat16)
    for k in (2, 1, 3):
        send(own, own, out_sem.at[n_tp - k], tp_peer[k])
    for k in (1, 3, 2):
        start = pl.multiple_of(((tp + k) % n_tp) * block, block)
        arrived(out_ref.at[pl.ds(start, block)], out_sem.at[k])
    for copy in sent:
        copy.wait_send()


def run_layer(queries, kv, table, starts, hidden, norm_moe, w_out, w_gate, w_up, w_down):
    tokens, width = hidden.shape
    n_tp = lax.axis_size("tp")
    n_seq = lax.axis_size("seq")
    block = tokens // n_tp
    slots, _, units = w_gate.shape
    lanes = queries.shape[1]
    bf16, f32 = jnp.bfloat16, jnp.float32
    flops = 2 * n_seq * tokens * slots * width * units * 3
    return pl.pallas_call(
        layer_kernel,
        out_shape=jax.ShapeDtypeStruct((tokens, width), bf16),
        in_specs=[pl.BlockSpec(memory_space=pltpu.VMEM)] * 4
        + [pl.BlockSpec(memory_space=pl.ANY), pl.BlockSpec(memory_space=pltpu.VMEM)]
        + [pl.BlockSpec(memory_space=pl.ANY)] * 4,
        out_specs=pl.BlockSpec(memory_space=pltpu.VMEM),
        scratch_shapes=[
            pltpu.VMEM((n_seq, 2, tokens // 2, kv.shape[1]), bf16),
            pltpu.VMEM((n_seq, 2, tokens // 2, table.shape[1]), bf16),
            pltpu.VMEM((block, width), bf16),
            pltpu.VMEM((queries.shape[0], 1), f32),
            pltpu.VMEM((queries.shape[0], 2 * lanes), f32),
            pltpu.VMEM((n_tp * w_out.shape[0], width), bf16),
            pltpu.VMEM((tokens, w_out.shape[0]), bf16),
            pltpu.VMEM((n_tp, block, w_out.shape[0]), bf16),
            pltpu.VMEM((block, width), bf16),
            pltpu.SemaphoreType.DMA((n_seq, 2)),
            pltpu.SemaphoreType.DMA((n_seq, 2)),
            pltpu.SemaphoreType.DMA((n_seq, n_tp)),
            pltpu.SemaphoreType.DMA((n_tp,)),
            pltpu.VMEM((n_seq, n_tp, block, width), bf16),
            pltpu.VMEM((slots, width, 2 * units), bf16),
            pltpu.VMEM((slots * units, width), bf16),
            pltpu.VMEM((tokens, slots * units), bf16),
            pltpu.VMEM((n_seq, n_tp, block, width), bf16),
            pltpu.VMEM((n_seq // 2, n_tp, block, width), bf16),
            pltpu.VMEM((2, n_tp, block, width), bf16),
            pltpu.VMEM((n_tp, block, width), bf16),
            pltpu.VMEM((n_tp, block, width), bf16),
            pltpu.SemaphoreType.DMA((2 * slots + 3,)),
            pltpu.SemaphoreType.DMA((144,)),
            pltpu.SemaphoreType.DMA((n_seq, n_tp)),
            pltpu.SemaphoreType.DMA((n_seq // 2,)),
            pltpu.SemaphoreType.DMA((2, n_tp)),
            pltpu.SemaphoreType.DMA((n_tp,)),
            pltpu.SemaphoreType.DMA((n_tp,)),
            pltpu.SemaphoreType.DMA((n_tp,)),
        ],
        compiler_params=pltpu.CompilerParams(
            collective_id=0, has_side_effects=True, vmem_limit_bytes=48 * 1024 * 1024
        ),
        cost_estimate=pl.CostEstimate(
            flops=flops, bytes_accessed=4 * 1024 * 1024, transcendentals=0
        ),
        name="layer",
    )(
        queries,
        kv,
        table,
        starts,
        hidden,
        norm_moe,
        w_out,
        w_gate,
        w_up,
        w_down.reshape(slots * units, width),
    )


def per_device(
    hidden,
    segment_ids,
    routes,
    gates,
    norm_attn,
    norm_moe,
    w_query,
    w_key,
    w_value,
    w_out,
    w_gate,
    w_up,
    w_down,
):
    tokens, width = hidden.shape
    queries, key_rot, value_proj, kv_cache, own_segs, query_index, starts = attention_inputs(
        hidden, segment_ids, norm_attn, w_query, w_key, w_value
    )
    table = expert_gates(routes, gates, EXPERTS)
    high = table.astype(jnp.bfloat16)
    low = (table - high.astype(jnp.float32)).astype(jnp.bfloat16)
    fill = jnp.zeros((tokens, 128 - 2 * EXPERTS), jnp.bfloat16)
    table = jnp.concatenate([high, low, fill], axis=1)
    kv_heads = key_rot.shape[1] // HEAD_DIM
    group_size = queries.shape[1] // kv_heads
    same = jnp.eye(kv_heads, dtype=jnp.bool_)
    queries = queries.transpose(1, 0, 2).reshape(kv_heads, group_size, tokens, 1, HEAD_DIM)
    queries = jnp.where(same[:, None, None, :, None], queries * SCORE_SCALE, 0).reshape(
        kv_heads * group_size * tokens, kv_heads * HEAD_DIM
    )
    out_rows = w_out.reshape(kv_heads, group_size, HEAD_DIM, width).transpose(1, 0, 2, 3)
    out_rows = out_rows.reshape(w_out.shape)
    kv = jnp.concatenate([key_rot, value_proj], axis=1)
    hidden_out = run_layer(
        queries,
        kv,
        table,
        starts[:, None],
        hidden,
        norm_moe[None, :],
        out_rows,
        w_gate,
        w_up,
        w_down,
    )
    return hidden_out, kv_cache


def solution(mesh):
    whole_rows = mesh.shape["seq"] == 8 and mesh.shape["tp"] == 4
    return jax.shard_map(
        per_device if whole_rows else per_device_routed,
        mesh=mesh,
        in_specs=(
            P("seq", None),
            P(),
            P("seq", None),
            P("seq", None),
            P(),
            P(),
            P(None, "tp"),
            P(None, "tp"),
            P(None, "tp"),
            P("tp", None),
            P("seq", None, "tp"),
            P("seq", None, "tp"),
            P("seq", "tp", None),
        ),
        out_specs=(P("seq", None), P("seq", None, "tp")),
        check_vma=False,
    )
```
